128 devices in a mesh: island: 8 (over y, core), fsdp: 16 (over z, x).
Axes of the slice: x: 4, y: 4, z: 4, core: 2. Of those that a mesh axis runs over, the one named last changes fastest.
Arguments:
- delta: bfloat16 [8, 5120, 2560], P('island', 'fsdp'), may hold values from -6 to 6
- error: bfloat16 [8, 5120, 2560], P('island', 'fsdp'), may hold values from -4 to 4
- params: float32 [5120, 2560], P('fsdp'), may hold values from -6 to 6
- momentum: float32 [5120, 2560], P('fsdp'), may hold values from -4 to 4
- q_init: float32 [2560, 64], replicated, may hold values from -6 to 6
- inputs: bfloat16 [65536, 5120], P(('island', 'fsdp')), may hold values from -0.078125 to 0.078125
Outputs:
- new_params: float32 [5120, 2560], P('fsdp')
- new_momentum: float32 [5120, 2560], P('fsdp')
- new_error: bfloat16 [8, 5120, 2560], P('island', 'fsdp')
- outputs: bfloat16 [65536, 2560], P(('island', 'fsdp'))
The draws below stay inside these ranges and needn't reach their ends.
All inputs are finite; a program needn't handle non-finite values.
Results may differ from the reference program's by a relative error of at most 0.0049.
Values may be sent and summed in bfloat16 or wider, within the bound.
A program may use at most 128 MiB of HBM per device.

```python
import jax
import jax.numpy as jnp
from jax import lax

D = 5120
COLS = 2560
RANK = 64
ISLANDS = 8
TOKENS = 65536


def block_scale(key, shape, cuts, least, largest):
    def one(dim, parts):
        steps = jax.random.uniform(jax.random.fold_in(jax.random.fold_in(key, 6), dim), (parts,), jnp.float32, least / len(cuts), largest / len(cuts))
        return jnp.repeat(jnp.exp(steps), shape[dim] // parts).reshape((-1,) + (1,) * (len(shape) - dim - 1))

    loudness = one(*cuts[0])
    for cut in cuts[1:]:
        loudness = loudness * one(*cut)
    return loudness


def scatter_about(key, shape, deviation, reach, shards=(), kind=jnp.bfloat16):
    values = jax.random.normal(key, shape, jnp.float32) * deviation
    if len(shards) > 0:
        values = block_scale(key, shape, shards, -0.22, 0.18) * values
    return jnp.clip(values, min=-reach, max=reach).astype(kind)


def setup_inputs(seed: int = 0) -> dict:
    splits = jax.random.split(jax.random.key(seed), 7)
    delta = scatter_about(splits[0], (ISLANDS, D, COLS), 1.0, 6.0, ((0, 8), (1, 16)))
    error = scatter_about(splits[1], (ISLANDS, D, COLS), 0.5, 4.0, ((0, 8), (1, 16)))
    params = scatter_about(splits[2], (D, COLS), 1.0, 6.0, ((0, 16),), jnp.float32)
    momentum = scatter_about(splits[3], (D, COLS), 0.5, 4.0, ((0, 16),), jnp.float32)
    q_init = scatter_about(splits[4], (COLS, RANK), 1.0, 6.0, (), jnp.float32)
    inputs = scatter_about(splits[5], (TOKENS, D), D ** -0.5, 0.078125, ((0, 128),))
    return dict(delta=delta, error=error, params=params, momentum=momentum, q_init=q_init, inputs=inputs)


def reference(delta, error, params, momentum, q_init, inputs):
    highest = lax.Precision.HIGHEST
    merged = delta.astype(jnp.float32) + error.astype(jnp.float32)
    p_sum = jnp.einsum('kdc,cr->dr', merged, q_init, precision=highest)
    gram = jnp.dot(p_sum.T, p_sum, precision=highest)
    lower = jnp.linalg.cholesky(gram)
    p_hat = jax.scipy.linalg.solve_triangular(lower, p_sum.T, lower=True).T
    q_sum = jnp.einsum('kdc,dr->cr', merged, p_hat, precision=highest)
    approx = jnp.dot(p_hat, q_sum.T, precision=highest) / ISLANDS
    new_error = (merged - approx[None]).astype(jnp.bfloat16)
    new_momentum = 0.9 * momentum + approx
    new_params = params - 0.7 * (approx + 0.9 * new_momentum)
    weights = new_params.astype(jnp.bfloat16)
    outputs = jnp.dot(inputs.astype(jnp.float32), weights.astype(jnp.float32), preferred_element_type=jnp.float32).astype(jnp.bfloat16)
    return (new_params, new_momentum, new_error, outputs)
```

```python
import jax
import jax.numpy as jnp
from jax import lax
from jax.sharding import PartitionSpec as P


def body(delta, error, params, momentum, q_init, inputs):
    highest = lax.Precision.HIGHEST
    islands = lax.axis_size("island")
    base = params - 0.567 * momentum
    gathered = lax.all_gather(base.astype(jnp.bfloat16), "fsdp", axis=0, tiled=True)
    merged = delta[0].astype(jnp.float32) + error[0].astype(jnp.float32)
    p_sum = lax.psum(jnp.dot(merged, q_init, precision=highest), "island")
    p_all = lax.all_gather(p_sum, "fsdp", axis=0, tiled=True)
    raw = jnp.dot(p_sum.T, merged, precision=highest)
    raw = lax.psum(raw, ("island", "fsdp"))
    gram = jnp.dot(p_all.T, p_all, precision=highest)
    lower = jnp.linalg.cholesky(gram)
    half = jax.scipy.linalg.solve_triangular(lower, raw, lower=True)
    right = jax.scipy.linalg.solve_triangular(lower, half, lower=True, trans=1) / islands
    approx = jnp.dot(p_sum, right, precision=highest)
    new_error = (merged - approx).astype(jnp.bfloat16)[None]
    new_momentum = 0.9 * momentum + approx
    new_params = params - 0.7 * (approx + 0.9 * new_momentum)
    high = p_all.astype(jnp.bfloat16)
    low = (p_all - high.astype(jnp.float32)).astype(jnp.bfloat16)
    left = jnp.dot(inputs, jnp.concatenate([high, low], axis=1), preferred_element_type=jnp.float32)
    left = left[:, :64] + left[:, 64:]
    total = jnp.dot(inputs, gathered, preferred_element_type=jnp.float32)
    total = total - 1.33 * jnp.dot(left, right, precision=highest)
    return (new_params, new_momentum, new_error, total.astype(jnp.bfloat16))


def solution(mesh):
    in_specs = (
        P("island", "fsdp", None),
        P("island", "fsdp", None),
        P("fsdp", None),
        P("fsdp", None),
        P(),
        P(("island", "fsdp"), None),
    )
    out_specs = (
        P("fsdp", None),
        P("fsdp", None),
        P("island", "fsdp", None),
        P(("island", "fsdp"), None),
    )
    return jax.shard_map(body, mesh=mesh, in_specs=in_specs, out_specs=out_specs, check_vma=False)
```

```python
import jax
import jax.numpy as jnp
from jax import lax
from jax.experimental import pallas as pl
from jax.experimental.pallas import tpu as pltpu
from jax.sharding import PartitionSpec as P

BF = jnp.bfloat16
F32 = jnp.float32
MESH = pl.DeviceIdType.MESH

ROWS = 320
HALF = 1280
UNIT = 640
STREAM = 112
CROSS = 48
WIDE = 1536
ROUNDS = 15
OFFS = (0, -1, 1, 2)


def plan():
    table = [[None] * 4 for _ in range(ROUNDS)]
    for side, (h0, h1, back) in enumerate(((0, 1, -1), (1, 0, 1))):
        x, z = side, 2 + side
        table[0][x], table[1][x], table[2][x] = ("a", 0, 0, h0), ("a", 0, 0, h1), ("a", back, 0, h0)
        table[0][z], table[1][z], table[2][z] = ("b", 0, 0, h0), ("b", 0, 0, h1), ("b", 0, back, h0)
        for k, off in enumerate(OFFS):
            table[3 + 3 * k][x] = ("b", 0, off, h0)
            table[4 + 3 * k][x] = ("b", 0, off, h1)
            table[5 + 3 * k][x] = ("b", back, off, h0)
            table[3 + 2 * k][z] = ("a", off, 0, h0)
            table[4 + 2 * k][z] = ("a", off, 0, h1)
            table[11 + k][z] = ("a", off, back, h0)
    return table


TABLE = plan()
UP = [(1, -1, 0), (1, 1, 0), (2, 2, 0)]
for _k, _o in enumerate(OFFS):
    UP += [(4 + 2 * _k, _o, -1), (4 + 2 * _k, _o, 1)]
UP += [(11 + _k, _o, 2) for _k, _o in enumerate(OFFS)]
DOWN = [(1, 0, -1), (1, 0, 1), (2, 0, 2)]
for _k, _o in enumerate(OFFS):
    DOWN += [(4 + 3 * _k, -1, _o), (4 + 3 * _k, 1, _o), (5 + 3 * _k, 2, _o)]


def kernel(
    delta, error, params, momentum, q_init, inputs,
    new_params, new_momentum, new_error, outputs,
    wbuf, xin, acc, dl, er, prm, mom, q32, q2, obuf, sbuf,
    ploc, ph1, ph2, pk, p2cat, pgb, pfull, tacc, tcat,
    rloc, rin, racc, yin, s16, t16, xrs, zrs, rfull, wf, wcat,
    plane_send, plane_recv, cross_send, cross_recv, load, store,
    c_send, c_recv, in_send, in_recv, out_send, out_recv,
):
    i, f = lax.axis_index("island"), lax.axis_index("fsdp")
    y, c = i // 2, lax.rem(i, 2)
    z, x = f // 4, lax.rem(f, 4)
    parity = lax.rem(y, 2)

    def wrap(v):
        return lax.rem(v + 4, 4)

    def peer(dx=0, dy=0, dz=0, dc=0):
        return (wrap(y + dy) * 2 + lax.rem(c + dc, 2), wrap(z + dz) * 4 + wrap(x + dx))

    def shard(dx, dz):
        return wrap(z + dz) * 4 + wrap(x + dx)

    PEERS = [dict(dx=1), dict(dx=-1), dict(dx=2), dict(dy=1), dict(dy=-1), dict(dy=2),
             dict(dz=1), dict(dz=-1), dict(dz=2), dict(dc=1)]
    LINKS = [dict(dx=1), dict(dx=-1), dict(dz=1), dict(dz=-1)]

    barrier = pltpu.get_barrier_semaphore()
    for p in PEERS:
        pl.semaphore_signal(barrier, inc=1, device_id=peer(**p), device_id_type=MESH)

    def mine(col):
        return pl.ds(pl.multiple_of(col, 128), HALF)

    loads = {}

    def start_load(n, src, dst):
        loads[n] = pltpu.make_async_copy(src, dst, load.at[n])
        loads[n].start()

    start_load(0, params.at[:, mine(c * HALF)], prm.at[c])
    start_load(1, momentum.at[:, mine(c * HALF)], mom.at[c])
    start_load(2, q_init, q32)
    start_load(3, delta.at[0], dl)
    start_load(4, error.at[0], er)
    start_load(5, inputs, xin.at[c])
    start_load(6, params.at[:, mine((1 - c) * HALF)], prm.at[1 - c])
    start_load(7, momentum.at[:, mine((1 - c) * HALF)], mom.at[1 - c])

    loads[0].wait()
    loads[1].wait()

    @pl.loop(0, ROWS // 32)
    def _(t):
        r = pl.ds(pl.multiple_of(t * 32, 32), 32)
        b = prm[c, r, :] - 0.567 * mom[c, r, :]
        wbuf[pl.ds(pl.multiple_of(f * ROWS + t * 32, 32), 32), :] = b.astype(BF)

    pl.semaphore_wait(barrier, len(PEERS))

    def region(stream, dx, dz, h):
        row = shard(dx, dz) * ROWS + CROSS * parity + (0 if stream == "a" else 160)
        return wbuf.at[pl.ds(pl.multiple_of(row, 16), STREAM), pl.ds(h * UNIT, UNIT)]

    def plane_copy(r, k, arriving=False):
        stream, dx, dz, h = TABLE[r][k]
        if arriving:
            step = -1 if k % 2 == 0 else 1
            dx, dz = (dx + step, dz) if k < 2 else (dx, dz + step)
        here = region(stream, dx, dz, h)
        return pltpu.make_async_remote_copy(
            src_ref=here, dst_ref=here, send_sem=plane_send.at[r, k], recv_sem=plane_recv.at[r, k],
            device_id=peer(**LINKS[k]), device_id_type=MESH)

    def cross_copy(way, j, arriving=False):
        _, dx, dz = (UP, DOWN)[way][j]
        par = 1 - parity if arriving else parity
        row = shard(dx, dz) * ROWS + 160 * way + 112 * par
        here = wbuf.at[pl.ds(pl.multiple_of(row, 16), CROSS), :]
        return pltpu.make_async_remote_copy(
            src_ref=here, dst_ref=here, send_sem=cross_send.at[way, j], recv_sem=cross_recv.at[way, j],
            device_id=peer(dy=1 if way == 0 else -1), device_id_type=MESH)

    def issue(r):
        for k in range(4):
            plane_copy(r, k).start()

    def service(q):
        for k in range(4):
            plane_copy(q, k, arriving=True).wait_recv()
        if q + 2 < ROUNDS:
            issue(q + 2)
        for way in range(2):
            for j, (need, _, _) in enumerate((UP, DOWN)[way]):
                if need == q:
                    cross_copy(way, j).start()

    def crossed(way, *js):
        for j in js:
            cross_copy(way, j, arriving=True).wait_recv()

    issue(0)
    issue(1)

    sent = []

    def send(n, src, dst, **to):
        copy = pltpu.make_async_remote_copy(
            src_ref=src, dst_ref=dst, send_sem=c_send.at[n], recv_sem=c_recv.at[n],
            device_id=peer(**to), device_id_type=MESH)
        copy.start()
        sent.append(copy)

    def arrive(n, dst):
        pltpu.make_async_remote_copy(
            src_ref=dst, dst_ref=dst, send_sem=c_send.at[n], recv_sem=c_recv.at[n],
            device_id=peer(dc=1), device_id_type=MESH).wait_recv()

    TO = (1, -1, 2)

    def swap(v):
        return pltpu.roll(v, 64, 1)

    loads[2].wait()

    v = q32[...]
    hi = v.astype(BF)
    q2[0:64, :] = hi
    q2[64:128, :] = (v - hi.astype(F32)).astype(BF)
    loads[3].wait()
    loads[4].wait()
    last_dims = (((1,), (1,)), ((), ()))
    p_loc = lax.dot_general(dl[...], q2[...], last_dims, preferred_element_type=F32)
    p_loc = p_loc + lax.dot_general(er[...], q2[...], last_dims, preferred_element_type=F32)
    p_loc = p_loc + swap(p_loc)
    low_lane = lax.broadcasted_iota(jnp.int32, (160, 128), 1) < 64
    ploc[...] = jnp.where(low_lane, p_loc[0:160], p_loc[160:320])

    def part(ref, k):
        return ref.at[pl.ds(pl.multiple_of(k * 80, 16), 80)]

    send(0, part(ploc, 1 - c), ph1, dc=1)

    in_copies = []

    def feed(k):
        rows = xin.at[c, pl.ds(k * 128, 128)]
        copy = pltpu.make_async_remote_copy(
            src_ref=rows, dst_ref=rows, send_sem=in_send.at[k], recv_sem=in_recv.at[k],
            device_id=peer(dc=1), device_id_type=MESH)
        copy.start()
        in_copies.append(copy)

    def fed(k):
        rows = xin.at[1 - c, pl.ds(k * 128, 128)]
        pltpu.make_async_remote_copy(
            src_ref=rows, dst_ref=rows, send_sem=in_send.at[k], recv_sem=in_recv.at[k],
            device_id=peer(dc=1), device_id_type=MESH).wait_recv()

    arrive(0, ph1)
    ph2[y] = part(ploc, c)[...] + ph1[...]
    for n, d in enumerate(TO):
        send(1 + n, ph2.at[y], ph2.at[y], dy=d)
    loads[5].wait()
    feed(0)
    service(0)
    for n, d in enumerate(TO):
        arrive(1 + n, ph2.at[wrap(y - d)])
    mine_sum = (ph2[0] + ph2[1]) + (ph2[2] + ph2[3])
    part(pk, c)[...] = mine_sum
    pgb[c, f] = mine_sum.astype(BF)
    send(4, part(pk, c), part(pk, c), dc=1)
    for n, d in enumerate(TO):
        send(5 + n, pgb.at[c, f], pgb.at[c, f], dx=d)
    feed(1)
    arrive(4, part(pk, 1 - c))
    whole = pk[...]
    other = swap(whole)
    dup = jnp.concatenate([jnp.where(low_lane, whole, other), jnp.where(low_lane, other, whole)], axis=0)
    hi = dup.astype(BF)
    lo = dup - hi.astype(F32)
    lane320 = lax.broadcasted_iota(jnp.int32, (ROWS, 128), 1) < 64
    p2cat[:, 0:128] = hi
    p2cat[:, 128:256] = jnp.where(lane320, lo, 0.0).astype(BF)
    service(1)
    split = jnp.where(lane320, hi.astype(F32), lo).astype(BF)
    contract = (((0,), (0,)), ((), ()))
    gram = lax.dot_general(dup, jnp.where(lane320, dup, 0.0), contract, precision=lax.Precision.HIGHEST,
                           preferred_element_type=F32)[0:64] * 0.125
    for h in range(2):
        rloc[h, :, 1280:1408] = gram
        rloc[h, :, 1408:1536] = jnp.zeros((64, 128), F32)
    for h in range(2):

        @pl.loop(0, 5)
        def _(t):
            src = pl.ds(pl.multiple_of(h * HALF + t * 256, 256), 256)
            v = lax.dot_general(split, dl[:, src], contract, preferred_element_type=F32)
            v = v + lax.dot_general(split, er[:, src], contract, preferred_element_type=F32)
            rloc[h, :, pl.ds(pl.multiple_of(t * 256, 256), 256)] = v[0:64] + v[64:128]

    send(8, rloc.at[1 - c], rin, dc=1)
    feed(2)
    service(2)
    for n, d in enumerate(TO):
        arrive(5 + n, pgb.at[c, shard(-d, 0)])
    row4 = pl.ds(z * 4, 4)
    for n, d in enumerate(TO):
        send(9 + n, pgb.at[c, row4], pgb.at[c, row4], dz=d)
    arrive(8, rin)
    racc[...] = rloc[c] + rin[...]

    def rows16(k):
        return pl.ds(pl.multiple_of(k * 16, 16), 16)

    for n, d in enumerate(TO):
        send(12 + n, racc.at[rows16(wrap(y + d))], yin.at[n], dy=d)
    service(3)
    feed(3)
    for n in range(3):
        arrive(12 + n, yin.at[n])
    s16[...] = (racc[rows16(y), :] + yin[0]) + (yin[1] + yin[2])

    def block(ref, k):
        return ref.at[pl.ds(pl.multiple_of((k // 2) * 8, 8), 8), pl.ds(pl.multiple_of(lax.rem(k, 2) * 768, 128), 768)]

    for n, d in enumerate(TO):
        send(15 + n, block(s16, wrap(x + d)), xrs.at[n], dx=d)
    service(4)
    for n in range(3):
        arrive(15 + n, xrs.at[n])
    zrs[z] = (block(s16, x)[...] + xrs[0]) + (xrs[1] + xrs[2])
    for n, d in enumerate(TO):
        send(18 + n, zrs.at[z], zrs.at[z], dz=d)
    service(5)
    for n, d in enumerate(TO):
        arrive(18 + n, zrs.at[wrap(z - d)])
    block(t16, x)[...] = (zrs[0] + zrs[1]) + (zrs[2] + zrs[3])
    for n, d in enumerate(TO):
        send(21 + n, block(t16, x), block(t16, x), dx=d)
    for n, d in enumerate(TO):
        arrive(9 + n, pgb.at[c, pl.ds(wrap(z - d) * 4, 4)])
    send(24, pgb.at[c], pgb.at[c], dc=1)
    service(6)
    for n, d in enumerate(TO):
        arrive(21 + n, block(t16, wrap(x - d)))
    rfull[rows16(y), :] = t16[...]
    for n, d in enumerate(TO):
        send(25 + n, rfull.at[rows16(y)], rfull.at[rows16(y)], dy=d)

    def product(row, depth, first=False):
        ks = pl.ds(pl.multiple_of(row, 128), depth)

        for m in range(2):

            @pl.loop(0, 5)
            def _(n):
                ns = pl.ds(pl.multiple_of(n * 256, 256), 256)
                v = jnp.dot(xin[m, :, ks], wbuf[ks, ns], preferred_element_type=F32)
                if first:
                    acc[m, :, ns] = v
                else:
                    acc[m, :, ns] += v

    service(7)
    for k in range(4):
        fed(k)
    crossed(0, 0, 1, 2)
    crossed(1, 3, 4, 5)
    product(z * 1280, 1280, first=True)
    service(8)

    arrive(24, pgb.at[1 - c])

    @pl.loop(0, 16)
    def _(t):
        for h in range(2):
            v = pgb[h, t]
            pfull[pl.ds(pl.multiple_of(t * ROWS + h * 80, 16), 80), :] = v
            pfull[pl.ds(pl.multiple_of(t * ROWS + 160 + h * 80, 16), 80), :] = swap(v.astype(F32)).astype(BF)

    for m in range(2):
        for k in range(4):
            v = jnp.dot(xin[m, :, k * 1280 : (k + 1) * 1280], pfull[k * 1280 : (k + 1) * 1280, :],
                        preferred_element_type=F32)
            if k == 0:
                tacc[m] = v
            else:
                tacc[m] += v
    lane512 = lax.broadcasted_iota(jnp.int32, (512, 128), 1) < 64
    for m in range(2):
        v = tacc[m] * -1.33
        v = jnp.where(lane512, v, swap(v))
        hi = v.astype(BF)
        tcat[m, :, 0:128] = hi
        tcat[m, :, 128:256] = jnp.where(lane512, v - hi.astype(F32), 0.0).astype(BF)
    service(9)

    for n, d in enumerate(TO):
        arrive(25 + n, rfull.at[rows16(wrap(y - d))])
    lane64 = lax.broadcasted_iota(jnp.int32, (64, 128), 1)
    sub64 = lax.broadcasted_iota(jnp.int32, (64, 128), 0)
    a = jnp.where(lane64 == sub64 + 64, 1.0, jnp.where(lane64 < 64, rfull[:, 1280:1408], 0.0))
    for k in range(64):
        row = a[k : k + 1, :] / a[k : k + 1, k : k + 1]
        a = jnp.where(sub64 == k, row, a - a[:, k : k + 1] * row)
    inverse = swap(a)[:, 0:64]
    wf[c] = jnp.dot(inverse, rfull[:, 0:1280], precision=lax.Precision.HIGHEST, preferred_element_type=F32) * 0.125
    send(28, wf.at[c], wf.at[c], dc=1)
    service(10)
    arrive(28, wf.at[1 - c])
    for h in range(2):
        v = wf[h]
        hi = v.astype(BF)
        wcat[h, 0:64, :] = hi
        wcat[h, 64:128, :] = (v - hi.astype(F32)).astype(BF)
        wcat[h, 128:192, :] = hi
        wcat[h, 192:256, :] = jnp.zeros((64, HALF), BF)

    loads[6].wait()
    loads[7].wait()
    for h in range(2):

        @pl.loop(0, ROWS // 32)
        def _(t):
            r = pl.ds(pl.multiple_of(t * 32, 32), 32)
            cols = slice(h * HALF, (h + 1) * HALF)
            approx = jnp.dot(p2cat[r, :], wcat[h], preferred_element_type=F32)
            merged = dl[r, cols].astype(F32) + er[r, cols].astype(F32)
            dl[r, cols] = (merged - approx).astype(BF)
            m = 0.9 * mom[h, r, :] + approx
            mom[h, r, :] = m
            prm[h, r, :] = prm[h, r, :] - 0.7 * (approx + 0.9 * m)

    stores = []

    def start_store(src, dst):
        copy = pltpu.make_async_copy(src, dst, store.at[len(stores)])
        copy.start()
        stores.append(copy)

    start_store(dl, new_error.at[0])
    for h in range(2):
        start_store(prm.at[h], new_params.at[:, pl.ds(h * HALF, HALF)])
        start_store(mom.at[h], new_momentum.at[:, pl.ds(h * HALF, HALF)])

    service(11)
    crossed(0, 3, 5, 7, 9)
    crossed(1, 0, 6, 7, 8)
    product(wrap(z - 1) * 1280, 1280)
    service(12)
    crossed(0, 4, 6, 8, 10)
    crossed(1, 1, 9, 10, 11)
    product(wrap(z + 1) * 1280, 1280)
    service(13)
    for m in range(2):

        @pl.loop(0, 5)
        def _(n):
            ns = pl.ds(pl.multiple_of(n * 256, 256), 256)
            acc[m, :, ns] += jnp.dot(tcat[m], wcat[c, :, ns], preferred_element_type=F32)

    crossed(0, 11, 12, 13)
    crossed(1, 2, 12, 13)
    last = wrap(z + 2) * 1280
    pair = x // 2
    service(14)
    product(last + pair * 640, 640)
    crossed(0, 14)
    crossed(1, 14)
    ks = pl.ds(pl.multiple_of(last + (1 - pair) * 640, 128), 640)

    def final(m, n):
        ns = pl.ds(n * 256, 256)
        return (acc[m, :, ns] + jnp.dot(xin[m, :, ks], wbuf[ks, ns], preferred_element_type=F32)).astype(BF)

    outs = []
    for n in range(5):
        sbuf[:, n * 256 : (n + 1) * 256] = final(1 - c, n)
        copy = pltpu.make_async_remote_copy(
            src_ref=sbuf.at[:, pl.ds(n * 256, 256)], dst_ref=obuf.at[c, :, pl.ds(n * 256, 256)],
            send_sem=out_send.at[n], recv_sem=out_recv.at[n], device_id=peer(dc=1), device_id_type=MESH)
        copy.start()
        outs.append(copy)
    for n in range(5):
        obuf[c, :, n * 256 : (n + 1) * 256] = final(c, n)
    start_store(obuf.at[c], outputs.at[:, mine(c * HALF)])
    for n in range(5):
        there = obuf.at[1 - c, :, pl.ds(n * 256, 256)]
        pltpu.make_async_remote_copy(
            src_ref=there, dst_ref=there, send_sem=out_send.at[n], recv_sem=out_recv.at[n],
            device_id=peer(dc=1), device_id_type=MESH).wait_recv()
    start_store(obuf.at[1 - c], outputs.at[:, mine((1 - c) * HALF)])

    for copy in sent + in_copies + outs:
        copy.wait_send()
    for r in range(ROUNDS):
        for k in range(4):
            plane_copy(r, k).wait_send()
    for way in range(2):
        for j in range(15):
            cross_copy(way, j).wait_send()
    for copy in stores:
        copy.wait()


def body(delta, error, params, momentum, q_init, inputs):
    dma = pltpu.SemaphoreType.DMA
    v = pltpu.VMEM
    anywhere = pl.BlockSpec(memory_space=pl.ANY)
    return tuple(pl.pallas_call(
        kernel,
        name="outer_step",
        out_shape=[
            jax.ShapeDtypeStruct((ROWS, 2560), F32),
            jax.ShapeDtypeStruct((ROWS, 2560), F32),
            jax.ShapeDtypeStruct((1, ROWS, 2560), BF),
            jax.ShapeDtypeStruct((512, 2560), BF),
        ],
        in_specs=[anywhere] * 6,
        out_specs=[anywhere] * 4,
        scratch_shapes=[
            v((5120, HALF), BF), v((2, 512, 5120), BF), v((2, 512, HALF), F32),
            v((ROWS, 2560), BF), v((ROWS, 2560), BF), v((2, ROWS, HALF), F32), v((2, ROWS, HALF), F32),
            v((64, 2560), F32), v((128, 2560), BF), v((2, 512, HALF), BF), v((512, HALF), BF),
            v((160, 128), F32), v((80, 128), F32), v((4, 80, 128), F32), v((160, 128), F32), v((ROWS, 256), BF),
            v((2, 16, 80, 128), BF), v((5120, 128), BF), v((2, 512, 128), F32), v((2, 512, 256), BF),
            v((2, 64, WIDE), F32), v((64, WIDE), F32), v((64, WIDE), F32), v((3, 16, WIDE), F32), v((16, WIDE), F32), v((16, WIDE), F32),
            v((3, 8, 768), F32), v((4, 8, 768), F32), v((64, WIDE), F32), v((2, 64, HALF), F32), v((2, 256, HALF), BF),
            dma((ROUNDS, 4)), dma((ROUNDS, 4)), dma((2, 15)), dma((2, 15)), dma((8,)), dma((8,)),
            dma((29,)), dma((29,)), dma((4,)), dma((4,)), dma((5,)), dma((5,)),
        ],
        compiler_params=pltpu.CompilerParams(collective_id=0, has_side_effects=True, vmem_limit_bytes=60 * 2**20),
        cost_estimate=pl.CostEstimate(flops=15 * 10**9, bytes_accessed=30 * 10**6, transcendentals=0),
    )(delta, error, params, momentum, q_init.T, inputs))


def solution(mesh):
    in_specs = (
        P("island", "fsdp", None),
        P("island", "fsdp", None),
        P("fsdp", None),
        P("fsdp", None),
        P(),
        P(("island", "fsdp"), None),
    )
    out_specs = (
        P("fsdp", None),
        P("fsdp", None),
        P("island", "fsdp", None),
        P(("island", "fsdp"), None),
    )
    return jax.shard_map(body, mesh=mesh, in_specs=in_specs, out_specs=out_specs, check_vma=False)
```

```python
import jax
import jax.numpy as jnp
from jax import lax
from jax.experimental import pallas as pl
from jax.experimental.pallas import tpu as pltpu
from jax.sharding import PartitionSpec as P

BF = jnp.bfloat16
F32 = jnp.float32
MESH = pl.DeviceIdType.MESH

ROWS = 320
HALF = 1280
UNIT = 640
STREAM = 112
CROSS = 48
ROUNDS = 15
LINES = 64
VMEM_MIB = 60
OFFS = (0, -1, 1, 2)


def plan():
    table = [[None] * 4 for _ in range(ROUNDS)]
    for side, (h0, h1, back) in enumerate(((0, 1, -1), (1, 0, 1))):
        x, z = side, 2 + side
        table[0][x], table[1][x], table[2][x] = ("a", 0, 0, h0), ("a", 0, 0, h1), ("a", back, 0, h0)
        table[0][z], table[1][z], table[2][z] = ("b", 0, 0, h0), ("b", 0, 0, h1), ("b", 0, back, h0)
        for k, off in enumerate(OFFS):
            table[3 + 3 * k][x] = ("b", 0, off, h0)
            table[4 + 3 * k][x] = ("b", 0, off, h1)
            table[5 + 3 * k][x] = ("b", back, off, h0)
            table[3 + 2 * k][z] = ("a", off, 0, h0)
            table[4 + 2 * k][z] = ("a", off, 0, h1)
            table[11 + k][z] = ("a", off, back, h0)
    return table


TABLE = plan()
UP = [(1, -1, 0), (1, 1, 0), (2, 2, 0)]
for _k, _o in enumerate(OFFS):
    UP += [(4 + 2 * _k, _o, -1), (4 + 2 * _k, _o, 1)]
UP += [(11 + _k, _o, 2) for _k, _o in enumerate(OFFS)]
DOWN = [(1, 0, -1), (1, 0, 1), (2, 0, 2)]
for _k, _o in enumerate(OFFS):
    DOWN += [(4 + 3 * _k, -1, _o), (4 + 3 * _k, 1, _o), (5 + 3 * _k, 2, _o)]


def kernel(
    delta, error, params, momentum, q_init, inputs,
    left_out, right_out, outputs,
    wbuf, xin, acc, dl, er, prm, mom, q32, q2, obuf, sbuf,
    ploc, ph1, ph2, pk, p2cat, pgb, pfull, tcat,
    gx, gz, inverse, split, rloc, rin, racc, yin, s16, t16, xrs, zrs, rfull, wf, wcat,
    plane_send, plane_recv, cross_send, cross_recv, load, store,
    c_send, c_recv, in_send, in_recv, out_send, out_recv,
):
    i, f = lax.axis_index("island"), lax.axis_index("fsdp")
    y, c = i // 2, lax.rem(i, 2)
    z, x = f // 4, lax.rem(f, 4)
    parity = lax.rem(y, 2)
    u, v = x + c * (z - x), z + c * (x - z)

    def wrap(v):
        return lax.rem(v + 4, 4)

    def peer(dx=0, dy=0, dz=0, dc=0):
        return (wrap(y + dy) * 2 + lax.rem(c + dc, 2), wrap(z + dz) * 4 + wrap(x + dx))

    def along_u(d):
        return dict(dx=d * (1 - c), dz=d * c)

    def along_v(d):
        return dict(dx=d * c, dz=d * (1 - c))

    def shard(dx, dz):
        return wrap(z + dz) * 4 + wrap(x + dx)

    PEERS = [dict(dx=1), dict(dx=-1), dict(dx=2), dict(dy=1), dict(dy=-1), dict(dy=2),
             dict(dz=1), dict(dz=-1), dict(dz=2), dict(dc=1)]
    LINKS = [dict(dx=1), dict(dx=-1), dict(dz=1), dict(dz=-1)]

    barrier = pltpu.get_barrier_semaphore()
    for p in PEERS:
        pl.semaphore_signal(barrier, inc=1, device_id=peer(**p), device_id_type=MESH)

    def mine(col):
        return pl.ds(pl.multiple_of(col, 128), HALF)

    loads = {}

    def start_load(n, src, dst):
        loads[n] = pltpu.make_async_copy(src, dst, load.at[n])
        loads[n].start()

    start_load(0, params.at[:, mine(c * HALF)], prm)
    start_load(1, momentum.at[:, mine(c * HALF)], mom)
    start_load(2, q_init, q32)
    start_load(3, delta.at[0], dl)
    start_load(4, error.at[0], er)

    loads[0].wait()
    loads[1].wait()

    @pl.loop(0, ROWS // 32)
    def _(t):
        r = pl.ds(pl.multiple_of(t * 32, 32), 32)
        b = prm[r, :] - 0.567 * mom[r, :]
        wbuf[pl.ds(pl.multiple_of(f * ROWS + t * 32, 32), 32), :] = b.astype(BF)

    def swap(v):
        return pltpu.roll(v, 64, 1)

    def low(rows):
        return lax.broadcasted_iota(jnp.int32, (rows, 128), 1) < 64

    loads[2].wait()
    q = q32[...]
    hi = q.astype(BF)
    q2[0:64, :] = hi
    q2[64:128, :] = (q - hi.astype(F32)).astype(BF)
    loads[3].wait()
    loads[4].wait()
    last_dims = (((1,), (1,)), ((), ()))
    p_loc = lax.dot_general(dl[...], q2[...], last_dims, preferred_element_type=F32)
    p_loc = p_loc + lax.dot_general(er[...], q2[...], last_dims, preferred_element_type=F32)
    p_loc = p_loc + swap(p_loc)
    ploc[...] = jnp.where(low(160), p_loc[0:160], p_loc[160:320])

    pl.semaphore_wait(barrier, len(PEERS))

    sent = []

    def send(n, src, dst, **to):
        copy = pltpu.make_async_remote_copy(
            src_ref=src, dst_ref=dst, send_sem=c_send.at[n], recv_sem=c_recv.at[n],
            device_id=peer(**to), device_id_type=MESH)
        copy.start()
        sent.append(copy)

    def arrive(n, dst):
        pltpu.make_async_remote_copy(
            src_ref=dst, dst_ref=dst, send_sem=c_send.at[n], recv_sem=c_recv.at[n],
            device_id=peer(dc=1), device_id_type=MESH).wait_recv()

    TO = (1, -1, 2)

    def region(stream, dx, dz, h):
        row = shard(dx, dz) * ROWS + CROSS * parity + (0 if stream == "a" else 160)
        return wbuf.at[pl.ds(pl.multiple_of(row, 16), STREAM), pl.ds(h * UNIT, UNIT)]

    def plane_copy(r, k, arriving=False):
        stream, dx, dz, h = TABLE[r][k]
        if arriving:
            step = -1 if k % 2 == 0 else 1
            dx, dz = (dx + step, dz) if k < 2 else (dx, dz + step)
        here = region(stream, dx, dz, h)
        return pltpu.make_async_remote_copy(
            src_ref=here, dst_ref=here, send_sem=plane_send.at[r, k], recv_sem=plane_recv.at[r, k],
            device_id=peer(**LINKS[k]), device_id_type=MESH)

    def cross_copy(way, j, arriving=False):
        _, dx, dz = (UP, DOWN)[way][j]
        par = 1 - parity if arriving else parity
        row = shard(dx, dz) * ROWS + 160 * way + STREAM * par
        here = wbuf.at[pl.ds(pl.multiple_of(row, 16), CROSS), :]
        return pltpu.make_async_remote_copy(
            src_ref=here, dst_ref=here, send_sem=cross_send.at[way, j], recv_sem=cross_recv.at[way, j],
            device_id=peer(dy=1 if way == 0 else -1), device_id_type=MESH)

    def issue(r):
        for k in range(4):
            plane_copy(r, k).start()

    def cross(*js):
        for j in js:
            for way in range(2):
                cross_copy(way, j).start()

    def got(q):
        for k in range(4):
            plane_copy(q, k, arriving=True).wait_recv()

    def go(q, hold=False):
        if q + 2 < ROUNDS:
            issue(q + 2)
        if not hold:
            for way in range(2):
                for j, (need, _, _) in enumerate((UP, DOWN)[way]):
                    if need == q:
                        cross_copy(way, j).start()

    def crossed(way, *js):
        for j in js:
            cross_copy(way, j, arriving=True).wait_recv()

    def part(ref, k):
        return ref.at[pl.ds(pl.multiple_of(k * 80, 16), 80)]

    send(0, part(ploc, 1 - c), ph1, dc=1)
    issue(0)
    issue(1)
    start_load(5, inputs, xin.at[c])
    arrive(0, ph1)
    ph2[y] = part(ploc, c)[...] + ph1[...]
    for n, d in enumerate(TO):
        send(1 + n, ph2.at[y], ph2.at[y], dy=d)

    in_copies = []

    def feed(k):
        rows = xin.at[c, pl.ds(k * 128, 128)]
        copy = pltpu.make_async_remote_copy(
            src_ref=rows, dst_ref=rows, send_sem=in_send.at[k], recv_sem=in_recv.at[k],
            device_id=peer(dc=1), device_id_type=MESH)
        copy.start()
        in_copies.append(copy)

    def fed(k):
        rows = xin.at[1 - c, pl.ds(k * 128, 128)]
        pltpu.make_async_remote_copy(
            src_ref=rows, dst_ref=rows, send_sem=in_send.at[k], recv_sem=in_recv.at[k],
            device_id=peer(dc=1), device_id_type=MESH).wait_recv()

    loads[5].wait()
    feed(0)
    got(0)
    go(0)

    for n, d in enumerate(TO):
        arrive(1 + n, ph2.at[wrap(y - d)])
    mine_sum = (ph2[0] + ph2[1]) + (ph2[2] + ph2[3])
    part(pk, c)[...] = mine_sum
    own = v * 4 + u
    pgb[c, own] = mine_sum.astype(BF)
    send(4, part(pk, c), part(pk, c), dc=1)
    for n, d in enumerate(TO):
        send(5 + n, pgb.at[c, own], pgb.at[c, own], **along_u(d))
    arrive(4, part(pk, 1 - c))
    whole = pk[...]
    other = swap(whole)
    dup = jnp.concatenate([jnp.where(low(160), whole, other), jnp.where(low(160), other, whole)], axis=0)
    low320 = low(ROWS)
    hi = dup.astype(BF)
    lo = dup - hi.astype(F32)
    p2cat[:, 0:128] = hi
    p2cat[:, 128:256] = jnp.where(low320, lo, 0.0).astype(BF)
    gram = lax.dot_general(dup, dup, (((0,), (0,)), ((), ())), precision=lax.Precision.HIGHEST,
                           preferred_element_type=F32)
    gx[u] = jnp.where(low(32), gram[0:32], gram[32:64])
    for n, d in enumerate(TO):
        send(29 + n, gx.at[u], gx.at[u], **along_u(d))
    got(1)
    go(1, hold=True)
    cross(0)
    split[...] = jnp.where(low320, hi.astype(F32), lo).T.astype(BF)
    for h in range(2):
        for t in range(2):
            src = slice(h * HALF + t * 640, h * HALF + (t + 1) * 640)
            raw = jnp.dot(split[...], dl[:, src], preferred_element_type=F32)
            raw = raw + jnp.dot(split[...], er[:, src], preferred_element_type=F32)
            rloc[h, :, t * 640 : (t + 1) * 640] = raw[0:64] + raw[64:128]

    send(8, rloc.at[1 - c], rin, dc=1)
    feed(1)
    got(2)
    for n, d in enumerate(TO):
        arrive(29 + n, gx.at[wrap(u - d)])
    gz[v] = (gx[0] + gx[1]) + (gx[2] + gx[3])
    for n, d in enumerate(TO):
        send(32 + n, gz.at[v], gz.at[v], **along_v(d))
    for n, d in enumerate(TO):
        arrive(5 + n, pgb.at[c, v * 4 + wrap(u - d)])
    row4 = pl.ds(v * 4, 4)
    for n, d in enumerate(TO):
        send(9 + n, pgb.at[c, row4], pgb.at[c, row4], **along_v(d))
    go(2, hold=True)
    arrive(8, rin)
    racc[...] = rloc[c] + rin[...]

    def rows16(k):
        return pl.ds(pl.multiple_of(k * 16, 16), 16)

    for n, d in enumerate(TO):
        send(12 + n, racc.at[rows16(wrap(y + d))], yin.at[n], dy=d)
    cross(1, 2)
    feed(2)
    feed(3)
    got(3)
    for n, d in enumerate(TO):
        arrive(32 + n, gz.at[wrap(v - d)])
    gram = (gz[0] + gz[1]) + (gz[2] + gz[3])
    go(3)

    lane64 = lax.broadcasted_iota(jnp.int32, (64, 128), 1)
    sub64 = lax.broadcasted_iota(jnp.int32, (64, 128), 0)
    a = jnp.concatenate([gram, swap(gram)], axis=0)
    a = jnp.where(lane64 < 64, a, jnp.where(lane64 == sub64 + 64, 1.0, 0.0))

    def eliminate(a, first, end):
        for k in range(first, end):
            row = a[k : k + 1, :] / a[k : k + 1, k : k + 1]
            a = jnp.where(sub64 == k, row, a - a[:, k : k + 1] * row)
        return a

    a = eliminate(a, 0, 32)
    got(4)
    for n, d in enumerate(TO):
        arrive(9 + n, pgb.at[c, pl.ds(wrap(v - d) * 4, 4)])
    send(24, pgb.at[c], pgb.at[c], dc=1)
    go(4)
    a = eliminate(a, 32, 64)
    inverse[...] = swap(a)
    got(5)
    for n in range(3):
        arrive(12 + n, yin.at[n])
    s16[...] = (racc[rows16(y), :] + yin[0]) + (yin[1] + yin[2])

    def block(ref, k):
        return ref.at[pl.ds(pl.multiple_of((k // 2) * 8, 8), 8), pl.ds(pl.multiple_of(lax.rem(k, 2) * 640, 128), 640)]

    for n, d in enumerate(TO):
        send(15 + n, block(s16, wrap(u + d)), xrs.at[n], **along_u(d))
    go(5)

    arrive(24, pgb.at[1 - c])

    @pl.loop(0, 16)
    def _(t):
        for h in range(2):
            two = pgb[h, t]
            at = (t if h == 0 else lax.rem(t, 4) * 4 + t // 4) * ROWS + h * 80
            pfull[pl.ds(pl.multiple_of(at, 16), 80), :] = two
            pfull[pl.ds(pl.multiple_of(at + 160, 16), 80), :] = swap(two.astype(F32)).astype(BF)

    low512 = low(512)

    def left(m):
        part_m = jnp.dot(xin[m], pfull[...], preferred_element_type=F32) * -1.33
        part_m = jnp.where(low512, part_m, swap(part_m))
        hi = part_m.astype(BF)
        tcat[m, :, 0:128] = hi
        tcat[m, :, 128:256] = jnp.where(low512, part_m - hi.astype(F32), 0.0).astype(BF)

    def product(row, depth, m, first=False):
        ks = pl.ds(pl.multiple_of(row, 128), depth)
        term = jnp.dot(xin[m, :, ks], wbuf[ks, :], preferred_element_type=F32)
        if first:
            acc[m] = term
        else:
            acc[m] += term

    for k in range(4):
        fed(k)
    got(6)
    for n in range(3):
        arrive(15 + n, xrs.at[n])
    zrs[v] = (block(s16, u)[...] + xrs[0]) + (xrs[1] + xrs[2])
    for n, d in enumerate(TO):
        send(18 + n, zrs.at[v], zrs.at[v], **along_v(d))
    go(6)
    left(0)
    got(7)
    for n, d in enumerate(TO):
        arrive(18 + n, zrs.at[wrap(v - d)])
    block(t16, u)[...] = (zrs[0] + zrs[1]) + (zrs[2] + zrs[3])
    for n, d in enumerate(TO):
        send(21 + n, block(t16, u), block(t16, u), **along_u(d))
    go(7)
    left(1)
    got(8)
    for n, d in enumerate(TO):
        arrive(21 + n, block(t16, wrap(u - d)))
    rfull[rows16(y), :] = t16[...]
    for n, d in enumerate(TO):
        send(25 + n, rfull.at[rows16(y)], rfull.at[rows16(y)], dy=d)
    go(8)
    crossed(0, 0, 1, 2)
    crossed(1, 3, 4, 5)
    product(z * 1280, 1280, 0, first=True)
    got(9)
    go(9)
    product(z * 1280, 1280, 1, first=True)
    got(10)
    go(10)
    for n, d in enumerate(TO):
        arrive(25 + n, rfull.at[rows16(wrap(y - d))])

    wf[c] = jnp.dot(inverse[:, 0:64], rfull[...], precision=lax.Precision.HIGHEST, preferred_element_type=F32) * 0.125
    send(28, wf.at[c], wf.at[c], dc=1)
    got(11)
    go(11)
    crossed(0, 3, 5, 7, 9)
    crossed(1, 0, 6, 7, 8)
    product(wrap(z - 1) * 1280, 1280, 0)
    got(12)
    go(12)
    product(wrap(z - 1) * 1280, 1280, 1)
    arrive(28, wf.at[1 - c])
    for h in range(2):
        w = wf[h]
        hi = w.astype(BF)
        wcat[h, 0:64, :] = hi
        wcat[h, 64:128, :] = (w - hi.astype(F32)).astype(BF)
        wcat[h, 128:192, :] = hi
        wcat[h, 192:256, :] = jnp.zeros((64, HALF), BF)
    stores = []

    def start_store(src, dst):
        copy = pltpu.make_async_copy(src, dst, store.at[len(stores)])
        copy.start()
        stores.append(copy)

    start_store(p2cat, left_out)
    start_store(wcat, right_out)
    got(13)
    go(13)
    crossed(0, 4, 6, 8, 10)
    crossed(1, 1, 9, 10, 11)
    product(wrap(z + 1) * 1280, 1280, 0)
    got(14)
    go(14)
    product(wrap(z + 1) * 1280, 1280, 1)

    @pl.loop(0, 2)
    def _(m):
        acc[m] += jnp.dot(tcat[m], wcat[c], preferred_element_type=F32)

    crossed(0, 11, 12, 13)
    crossed(1, 2, 12, 13)
    last = wrap(z + 2) * 1280
    pair = x // 2
    for m in range(2):
        product(last + pair * 640, 640, m)
    crossed(0, 14)
    crossed(1, 14)
    ks = pl.ds(pl.multiple_of(last + (1 - pair) * 640, 128), 640)

    def final(m, t):
        rows = slice(t * 256, (t + 1) * 256)
        return (acc[m, rows, :] + jnp.dot(xin[m, rows, ks], wbuf[ks, :], preferred_element_type=F32)).astype(BF)

    outs = []
    for t in range(2):
        rows = pl.ds(t * 256, 256)
        sbuf[t * 256 : (t + 1) * 256, :] = final(1 - c, t)
        copy = pltpu.make_async_remote_copy(
            src_ref=sbuf.at[rows], dst_ref=obuf.at[c, rows],
            send_sem=out_send.at[t], recv_sem=out_recv.at[t], device_id=peer(dc=1), device_id_type=MESH)
        copy.start()
        outs.append(copy)
    for t in range(2):
        obuf[c, t * 256 : (t + 1) * 256, :] = final(c, t)
    start_store(obuf.at[c], outputs.at[:, mine(c * HALF)])
    for t in range(2):
        there = obuf.at[1 - c, pl.ds(t * 256, 256)]
        pltpu.make_async_remote_copy(
            src_ref=there, dst_ref=there, send_sem=out_send.at[t], recv_sem=out_recv.at[t],
            device_id=peer(dc=1), device_id_type=MESH).wait_recv()
    start_store(obuf.at[1 - c], outputs.at[:, mine((1 - c) * HALF)])

    for copy in sent + in_copies + outs:
        copy.wait_send()
    for r in range(ROUNDS):
        for k in range(4):
            plane_copy(r, k).wait_send()
    for way in range(2):
        for j in range(15):
            cross_copy(way, j).wait_send()
    for copy in stores:
        copy.wait()


def finish(delta, error, params, momentum, left, right, ready, new_params, new_momentum, new_error, outputs):
    outputs[...] = ready[...]
    for h in range(2):
        cols = slice(h * HALF, (h + 1) * HALF)
        approx = jnp.dot(left[...], right[h], preferred_element_type=F32)
        merged = delta[0, :, cols].astype(F32) + error[0, :, cols].astype(F32)
        new_error[0, :, cols] = (merged - approx).astype(BF)
        m = 0.9 * momentum[:, cols] + approx
        new_momentum[:, cols] = m
        new_params[:, cols] = params[:, cols] - 0.7 * (approx + 0.9 * m)


def body(delta, error, params, momentum, q_init, inputs):
    dma = pltpu.SemaphoreType.DMA
    v = pltpu.VMEM
    anywhere = pl.BlockSpec(memory_space=pl.ANY)
    left, right, ready = pl.pallas_call(
        kernel,
        name="outer_step",
        out_shape=[
            jax.ShapeDtypeStruct((ROWS, 256), BF),
            jax.ShapeDtypeStruct((2, 256, HALF), BF),
            jax.ShapeDtypeStruct((512, 2560), BF),
        ],
        in_specs=[anywhere] * 6,
        out_specs=[anywhere] * 3,
        scratch_shapes=[
            v((5120, HALF), BF), v((2, 512, 5120), BF), v((2, 512, HALF), F32),
            v((ROWS, 2560), BF), v((ROWS, 2560), BF), v((ROWS, HALF), F32), v((ROWS, HALF), F32),
            v((64, 2560), F32), v((128, 2560), BF), v((2, 512, HALF), BF), v((512, HALF), BF),
            v((160, 128), F32), v((80, 128), F32), v((4, 80, 128), F32), v((160, 128), F32), v((ROWS, 256), BF),
            v((2, 16, 80, 128), BF), v((5120, 128), BF), v((2, 512, 256), BF),
            v((4, 32, 128), F32), v((4, 32, 128), F32), v((64, 128), F32), v((128, ROWS), BF),
            v((2, 64, HALF), F32), v((64, HALF), F32), v((64, HALF), F32), v((3, 16, HALF), F32), v((16, HALF), F32), v((16, HALF), F32),
            v((3, 8, 640), F32), v((4, 8, 640), F32), v((64, HALF), F32), v((2, 64, HALF), F32), v((2, 256, HALF), BF),
            dma((ROUNDS, 4)), dma((ROUNDS, 4)), dma((2, 15)), dma((2, 15)), dma((8,)), dma((8,)),
            dma((35,)), dma((35,)), dma((4,)), dma((4,)), dma((2,)), dma((2,)),
        ],
        compiler_params=pltpu.CompilerParams(collective_id=0, has_side_effects=True, vmem_limit_bytes=VMEM_MIB * 2**20),
        cost_estimate=pl.CostEstimate(flops=15 * 10**9, bytes_accessed=30 * 10**6, transcendentals=0),
    )(delta, error, params, momentum, q_init.T, inputs)
    lines = pl.BlockSpec((LINES, 2560), lambda i: (i, 0))
    columns = pl.BlockSpec((512, 8 * LINES), lambda i: (0, i))
    boxed = pl.BlockSpec((1, LINES, 2560), lambda i: (0, i, 0))
    return tuple(pl.pallas_call(
        finish,
        name="finish",
        grid=(ROWS // LINES,),
        out_shape=[
            jax.ShapeDtypeStruct((ROWS, 2560), F32),
            jax.ShapeDtypeStruct((ROWS, 2560), F32),
            jax.ShapeDtypeStruct((1, ROWS, 2560), BF),
            jax.ShapeDtypeStruct((512, 2560), BF),
        ],
        in_specs=[
            boxed, boxed, lines, lines, pl.BlockSpec((LINES, 256), lambda i: (i, 0)),
            pl.BlockSpec((2, 256, HALF), lambda i: (0, 0, 0)), columns,
        ],
        out_specs=[lines, lines, boxed, columns],
        compiler_params=pltpu.CompilerParams(vmem_limit_bytes=VMEM_MIB * 2**20),
        cost_estimate=pl.CostEstimate(flops=500 * 10**6, bytes_accessed=24 * 10**6, transcendentals=0),
    )(delta, error, params, momentum, left, right, ready))


def solution(mesh):
    in_specs = (
        P("island", "fsdp", None),
        P("island", "fsdp", None),
        P("fsdp", None),
        P("fsdp", None),
        P(),
        P(("island", "fsdp"), None),
    )
    out_specs = (
        P("fsdp", None),
        P("fsdp", None),
        P("island", "fsdp", None),
        P(("island", "fsdp"), None),
    )
    return jax.shard_map(body, mesh=mesh, in_specs=in_specs, out_specs=out_specs, check_vma=False)
```

```python
import jax
import jax.numpy as jnp
from jax import lax
from jax.experimental import pallas as pl
from jax.experimental.pallas import tpu as pltpu
from jax.sharding import PartitionSpec as P

BF = jnp.bfloat16
F32 = jnp.float32
MESH = pl.DeviceIdType.MESH

ROWS = 320
HALF = 1280
UNIT = 640
STREAM = 112
CROSS = 48
ROUNDS = 15
LINES = 160
VMEM_MIB = 60
OFFS = (0, -1, 1, 2)


def plan():
    table = [[None] * 4 for _ in range(ROUNDS)]
    for side, (h0, h1, back) in enumerate(((0, 1, -1), (1, 0, 1))):
        x, z = side, 2 + side
        table[0][x], table[1][x], table[2][x] = ("a", 0, 0, h0), ("a", 0, 0, h1), ("a", back, 0, h0)
        table[0][z], table[1][z], table[2][z] = ("b", 0, 0, h0), ("b", 0, 0, h1), ("b", 0, back, h0)
        for k, off in enumerate(OFFS):
            table[3 + 3 * k][x] = ("b", 0, off, h0)
            table[4 + 3 * k][x] = ("b", 0, off, h1)
            table[5 + 3 * k][x] = ("b", back, off, h0)
            table[3 + 2 * k][z] = ("a", off, 0, h0)
            table[4 + 2 * k][z] = ("a", off, 0, h1)
            table[11 + k][z] = ("a", off, back, h0)
    return table


TABLE = plan()
UP = [(1, -1, 0), (1, 1, 0), (2, 2, 0)]
for _k, _o in enumerate(OFFS):
    UP += [(4 + 2 * _k, _o, -1), (4 + 2 * _k, _o, 1)]
UP += [(11 + _k, _o, 2) for _k, _o in enumerate(OFFS)]
DOWN = [(1, 0, -1), (1, 0, 1), (2, 0, 2)]
for _k, _o in enumerate(OFFS):
    DOWN += [(4 + 3 * _k, -1, _o), (4 + 3 * _k, 1, _o), (5 + 3 * _k, 2, _o)]


def kernel(
    delta, error, params, momentum, q_init, inputs,
    left_out, right_out, outputs,
    wbuf, xin, acc, dl, er, prm, mom, q32, q2, obuf, sbuf,
    ploc, ph1, ph2, pk, p2cat, pgb, pfull, tcat,
    gx, gz, inverse, split, rloc, rin, racc, yin, s16, t16, xrs, zrs, rfull, wf, wcat,
    plane_send, plane_recv, cross_send, cross_recv, load, store,
    c_send, c_recv, in_send, in_recv, out_send, out_recv,
):
    i, f = lax.axis_index("island"), lax.axis_index("fsdp")
    y, c = i // 2, lax.rem(i, 2)
    z, x = f // 4, lax.rem(f, 4)
    parity = lax.rem(y, 2)
    u, v = x + c * (z - x), z + c * (x - z)

    def wrap(v):
        return lax.rem(v + 4, 4)

    def peer(dx=0, dy=0, dz=0, dc=0):
        return (wrap(y + dy) * 2 + lax.rem(c + dc, 2), wrap(z + dz) * 4 + wrap(x + dx))

    def along_u(d):
        return dict(dx=d * (1 - c), dz=d * c)

    def along_v(d):
        return dict(dx=d * c, dz=d * (1 - c))

    def shard(dx, dz):
        return wrap(z + dz) * 4 + wrap(x + dx)

    PEERS = [dict(dx=1), dict(dx=-1), dict(dx=2), dict(dy=1), dict(dy=-1), dict(dy=2),
             dict(dz=1), dict(dz=-1), dict(dz=2), dict(dc=1)]
    LINKS = [dict(dx=1), dict(dx=-1), dict(dz=1), dict(dz=-1)]

    barrier = pltpu.get_barrier_semaphore()
    for p in PEERS:
        pl.semaphore_signal(barrier, inc=1, device_id=peer(**p), device_id_type=MESH)

    def mine(col):
        return pl.ds(pl.multiple_of(col, 128), HALF)

    loads = {}

    def start_load(n, src, dst):
        loads[n] = pltpu.make_async_copy(src, dst, load.at[n])
        loads[n].start()

    start_load(0, params.at[:, mine(c * HALF)], prm)
    start_load(1, momentum.at[:, mine(c * HALF)], mom)
    start_load(2, q_init, q32)
    start_load(3, delta.at[0], dl)
    start_load(4, error.at[0], er)

    loads[0].wait()
    loads[1].wait()

    @pl.loop(0, ROWS // 32)
    def _(t):
        r = pl.ds(pl.multiple_of(t * 32, 32), 32)
        b = prm[r, :] - 0.567 * mom[r, :]
        wbuf[pl.ds(pl.multiple_of(f * ROWS + t * 32, 32), 32), :] = b.astype(BF)

    def swap(v):
        return pltpu.roll(v, 64, 1)

    def low(rows):
        return lax.broadcasted_iota(jnp.int32, (rows, 128), 1) < 64

    loads[2].wait()
    q = q32[...]
    hi = q.astype(BF)
    q2[0:64, :] = hi
    q2[64:128, :] = (q - hi.astype(F32)).astype(BF)
    loads[3].wait()
    loads[4].wait()
    last_dims = (((1,), (1,)), ((), ()))
    p_loc = lax.dot_general(dl[...], q2[...], last_dims, preferred_element_type=F32)
    p_loc = p_loc + lax.dot_general(er[...], q2[...], last_dims, preferred_element_type=F32)
    p_loc = p_loc + swap(p_loc)
    ploc[...] = jnp.where(low(160), p_loc[0:160], p_loc[160:320])

    pl.semaphore_wait(barrier, len(PEERS))

    sent = []

    def send(n, src, dst, **to):
        copy = pltpu.make_async_remote_copy(
            src_ref=src, dst_ref=dst, send_sem=c_send.at[n], recv_sem=c_recv.at[n],
            device_id=peer(**to), device_id_type=MESH)
        copy.start()
        sent.append(copy)

    def arrive(n, dst):
        pltpu.make_async_remote_copy(
            src_ref=dst, dst_ref=dst, send_sem=c_send.at[n], recv_sem=c_recv.at[n],
            device_id=peer(dc=1), device_id_type=MESH).wait_recv()

    TO = (1, -1, 2)

    def region(stream, dx, dz, h):
        row = shard(dx, dz) * ROWS + CROSS * parity + (0 if stream == "a" else 160)
        return wbuf.at[pl.ds(pl.multiple_of(row, 16), STREAM), pl.ds(h * UNIT, UNIT)]

    def plane_copy(r, k, arriving=False):
        stream, dx, dz, h = TABLE[r][k]
        if arriving:
            step = -1 if k % 2 == 0 else 1
            dx, dz = (dx + step, dz) if k < 2 else (dx, dz + step)
        here = region(stream, dx, dz, h)
        return pltpu.make_async_remote_copy(
            src_ref=here, dst_ref=here, send_sem=plane_send.at[r, k], recv_sem=plane_recv.at[r, k],
            device_id=peer(**LINKS[k]), device_id_type=MESH)

    def cross_copy(way, j, arriving=False):
        _, dx, dz = (UP, DOWN)[way][j]
        par = 1 - parity if arriving else parity
        row = shard(dx, dz) * ROWS + 160 * way + STREAM * par
        here = wbuf.at[pl.ds(pl.multiple_of(row, 16), CROSS), :]
        return pltpu.make_async_remote_copy(
            src_ref=here, dst_ref=here, send_sem=cross_send.at[way, j], recv_sem=cross_recv.at[way, j],
            device_id=peer(dy=1 if way == 0 else -1), device_id_type=MESH)

    def issue(r):
        for k in range(4):
            plane_copy(r, k).start()

    def cross(*js):
        for j in js:
            for way in range(2):
                cross_copy(way, j).start()

    def got(q):
        for k in range(4):
            plane_copy(q, k, arriving=True).wait_recv()

    def go(q, hold=False):
        if q + 2 < ROUNDS:
            issue(q + 2)
        if not hold:
            for way in range(2):
                for j, (need, _, _) in enumerate((UP, DOWN)[way]):
                    if need == q:
                        cross_copy(way, j).start()

    def crossed(way, *js):
        for j in js:
            cross_copy(way, j, arriving=True).wait_recv()

    def part(ref, k):
        return ref.at[pl.ds(pl.multiple_of(k * 80, 16), 80)]

    send(0, part(ploc, 1 - c), ph1, dc=1)
    issue(0)
    issue(1)
    start_load(5, inputs, xin.at[c])
    arrive(0, ph1)
    ph2[y] = part(ploc, c)[...] + ph1[...]
    for n, d in enumerate(TO):
        send(1 + n, ph2.at[y], ph2.at[y], dy=d)

    in_copies = []

    def feed(k):
        rows = xin.at[c, pl.ds(k * 128, 128)]
        copy = pltpu.make_async_remote_copy(
            src_ref=rows, dst_ref=rows, send_sem=in_send.at[k], recv_sem=in_recv.at[k],
            device_id=peer(dc=1), device_id_type=MESH)
        copy.start()
        in_copies.append(copy)

    def fed(k):
        rows = xin.at[1 - c, pl.ds(k * 128, 128)]
        pltpu.make_async_remote_copy(
            src_ref=rows, dst_ref=rows, send_sem=in_send.at[k], recv_sem=in_recv.at[k],
            device_id=peer(dc=1), device_id_type=MESH).wait_recv()

    loads[5].wait()
    feed(0)
    got(0)
    go(0)

    for n, d in enumerate(TO):
        arrive(1 + n, ph2.at[wrap(y - d)])
    mine_sum = (ph2[0] + ph2[1]) + (ph2[2] + ph2[3])
    part(pk, c)[...] = mine_sum
    own = v * 4 + u
    pgb[c, own] = mine_sum.astype(BF)
    send(4, part(pk, c), part(pk, c), dc=1)
    for n, d in enumerate(TO):
        send(5 + n, pgb.at[c, own], pgb.at[c, own], **along_u(d))
    arrive(4, part(pk, 1 - c))
    whole = pk[...]
    other = swap(whole)
    dup = jnp.concatenate([jnp.where(low(160), whole, other), jnp.where(low(160), other, whole)], axis=0)
    low320 = low(ROWS)
    hi = dup.astype(BF)
    lo = dup - hi.astype(F32)
    p2cat[:, 0:128] = hi
    p2cat[:, 128:256] = jnp.where(low320, lo, 0.0).astype(BF)
    gram = lax.dot_general(dup, dup, (((0,), (0,)), ((), ())), precision=lax.Precision.HIGHEST,
                           preferred_element_type=F32)
    gx[u] = jnp.where(low(32), gram[0:32], gram[32:64])
    for n, d in enumerate(TO):
        send(29 + n, gx.at[u], gx.at[u], **along_u(d))
    got(1)
    go(1, hold=True)
    cross(0)
    split[...] = jnp.where(low320, hi.astype(F32), lo).T.astype(BF)
    for h in range(2):
        for t in range(2):
            src = slice(h * HALF + t * 640, h * HALF + (t + 1) * 640)
            raw = jnp.dot(split[...], dl[:, src], preferred_element_type=F32)
            raw = raw + jnp.dot(split[...], er[:, src], preferred_element_type=F32)
            rloc[h, :, t * 640 : (t + 1) * 640] = raw[0:64] + raw[64:128]

    send(8, rloc.at[1 - c], rin, dc=1)
    feed(1)
    got(2)
    for n, d in enumerate(TO):
        arrive(29 + n, gx.at[wrap(u - d)])
    gz[v] = (gx[0] + gx[1]) + (gx[2] + gx[3])
    for n, d in enumerate(TO):
        send(32 + n, gz.at[v], gz.at[v], **along_v(d))
    for n, d in enumerate(TO):
        arrive(5 + n, pgb.at[c, v * 4 + wrap(u - d)])
    row4 = pl.ds(v * 4, 4)
    for n, d in enumerate(TO):
        send(9 + n, pgb.at[c, row4], pgb.at[c, row4], **along_v(d))
    go(2, hold=True)
    arrive(8, rin)
    racc[...] = rloc[c] + rin[...]

    def rows16(k):
        return pl.ds(pl.multiple_of(k * 16, 16), 16)

    for n, d in enumerate(TO):
        send(12 + n, racc.at[rows16(wrap(y + d))], yin.at[n], dy=d)
    cross(1, 2)
    feed(2)
    feed(3)
    got(3)
    for n, d in enumerate(TO):
        arrive(32 + n, gz.at[wrap(v - d)])
    gram = (gz[0] + gz[1]) + (gz[2] + gz[3])
    go(3)

    lane64 = lax.broadcasted_iota(jnp.int32, (64, 128), 1)
    sub64 = lax.broadcasted_iota(jnp.int32, (64, 128), 0)
    a = jnp.concatenate([gram, swap(gram)], axis=0)
    a = jnp.where(lane64 < 64, a, jnp.where(lane64 == sub64 + 64, 1.0, 0.0))

    def eliminate(a, first, end):
        for k in range(first, end):
            row = a[k : k + 1, :] / a[k : k + 1, k : k + 1]
            a = jnp.where(sub64 == k, row, a - a[:, k : k + 1] * row)
        return a

    a = eliminate(a, 0, 32)
    got(4)
    for n, d in enumerate(TO):
        arrive(9 + n, pgb.at[c, pl.ds(wrap(v - d) * 4, 4)])
    send(24, pgb.at[c], pgb.at[c], dc=1)
    go(4)
    a = eliminate(a, 32, 64)
    inverse[...] = swap(a)
    got(5)
    for n in range(3):
        arrive(12 + n, yin.at[n])
    s16[...] = (racc[rows16(y), :] + yin[0]) + (yin[1] + yin[2])

    def block(ref, k):
        return ref.at[pl.ds(pl.multiple_of((k // 2) * 8, 8), 8), pl.ds(pl.multiple_of(lax.rem(k, 2) * 640, 128), 640)]

    for n, d in enumerate(TO):
        send(15 + n, block(s16, wrap(u + d)), xrs.at[n], **along_u(d))
    go(5)

    arrive(24, pgb.at[1 - c])

    @pl.loop(0, 16)
    def _(t):
        for h in range(2):
            two = pgb[h, t]
            at = (t if h == 0 else lax.rem(t, 4) * 4 + t // 4) * ROWS + h * 80
            pfull[pl.ds(pl.multiple_of(at, 16), 80), :] = two
            pfull[pl.ds(pl.multiple_of(at + 160, 16), 80), :] = swap(two.astype(F32)).astype(BF)

    low512 = low(512)

    def left(m):
        part_m = jnp.dot(xin[m], pfull[...], preferred_element_type=F32) * -1.33
        part_m = jnp.where(low512, part_m, swap(part_m))
        hi = part_m.astype(BF)
        tcat[m, :, 0:128] = hi
        tcat[m, :, 128:256] = jnp.where(low512, part_m - hi.astype(F32), 0.0).astype(BF)

    def product(row, depth, m, first=False):
        ks = pl.ds(pl.multiple_of(row, 128), depth)
        term = jnp.dot(xin[m, :, ks], wbuf[ks, :], preferred_element_type=F32)
        if first:
            acc[m] = term
        else:
            acc[m] += term

    for k in range(4):
        fed(k)
    got(6)
    for n in range(3):
        arrive(15 + n, xrs.at[n])
    zrs[v] = (block(s16, u)[...] + xrs[0]) + (xrs[1] + xrs[2])
    for n, d in enumerate(TO):
        send(18 + n, zrs.at[v], zrs.at[v], **along_v(d))
    go(6)
    left(0)
    got(7)
    for n, d in enumerate(TO):
        arrive(18 + n, zrs.at[wrap(v - d)])
    block(t16, u)[...] = (zrs[0] + zrs[1]) + (zrs[2] + zrs[3])
    for n, d in enumerate(TO):
        send(21 + n, block(t16, u), block(t16, u), **along_u(d))
    go(7)
    left(1)
    got(8)
    for n, d in enumerate(TO):
        arrive(21 + n, block(t16, wrap(u - d)))
    rfull[rows16(y), :] = t16[...]
    for n, d in enumerate(TO):
        send(25 + n, rfull.at[rows16(y)], rfull.at[rows16(y)], dy=d)
    go(8)
    crossed(0, 0, 1, 2)
    crossed(1, 3, 4, 5)
    product(z * 1280, 1280, 0, first=True)
    got(9)
    go(9)
    product(z * 1280, 1280, 1, first=True)
    got(10)
    go(10)
    for n, d in enumerate(TO):
        arrive(25 + n, rfull.at[rows16(wrap(y - d))])

    wf[c] = jnp.dot(inverse[:, 0:64], rfull[...], precision=lax.Precision.HIGHEST, preferred_element_type=F32) * 0.125
    send(28, wf.at[c], wf.at[c], dc=1)
    got(11)
    go(11)
    arrive(28, wf.at[1 - c])
    for h in range(2):
        w = wf[h]
        hi = w.astype(BF)
        wcat[h, 0:64, :] = hi
        wcat[h, 64:128, :] = (w - hi.astype(F32)).astype(BF)
        wcat[h, 128:192, :] = hi
        wcat[h, 192:256, :] = jnp.zeros((64, HALF), BF)
    stores = []

    def start_store(src, dst):
        copy = pltpu.make_async_copy(src, dst, store.at[len(stores)])
        copy.start()
        stores.append(copy)

    start_store(p2cat, left_out)
    start_store(wcat, right_out)

    @pl.loop(0, 2)
    def _(m):
        acc[m] += jnp.dot(tcat[m], wcat[c], preferred_element_type=F32)

    got(12)
    go(12)
    crossed(0, 3, 5, 7, 9)
    crossed(1, 0, 6, 7, 8)
    product(wrap(z - 1) * 1280, 1280, 0)
    product(wrap(z - 1) * 1280, 1280, 1)
    got(13)
    go(13)
    crossed(0, 4, 6, 8, 10)
    crossed(1, 1, 9, 10, 11)
    product(wrap(z + 1) * 1280, 1280, 0)
    got(14)
    go(14)
    product(wrap(z + 1) * 1280, 1280, 1)

    crossed(0, 11, 12, 13)
    crossed(1, 2, 12, 13)
    last = wrap(z + 2) * 1280
    pair = x // 2
    for m in range(2):
        product(last + pair * 640, 640, m)
    crossed(0, 14)
    crossed(1, 14)
    ks = pl.ds(pl.multiple_of(last + (1 - pair) * 640, 128), 640)

    def final(m, t):
        rows = slice(t * 256, (t + 1) * 256)
        return (acc[m, rows, :] + jnp.dot(xin[m, rows, ks], wbuf[ks, :], preferred_element_type=F32)).astype(BF)

    outs = []
    for t in range(2):
        rows = pl.ds(t * 256, 256)
        sbuf[t * 256 : (t + 1) * 256, :] = final(1 - c, t)
        copy = pltpu.make_async_remote_copy(
            src_ref=sbuf.at[rows], dst_ref=obuf.at[c, rows],
            send_sem=out_send.at[t], recv_sem=out_recv.at[t], device_id=peer(dc=1), device_id_type=MESH)
        copy.start()
        outs.append(copy)
    for t in range(2):
        obuf[c, t * 256 : (t + 1) * 256, :] = final(c, t)
    start_store(obuf.at[c], outputs.at[:, mine(c * HALF)])
    for t in range(2):
        there = obuf.at[1 - c, pl.ds(t * 256, 256)]
        pltpu.make_async_remote_copy(
            src_ref=there, dst_ref=there, send_sem=out_send.at[t], recv_sem=out_recv.at[t],
            device_id=peer(dc=1), device_id_type=MESH).wait_recv()
    start_store(obuf.at[1 - c], outputs.at[:, mine((1 - c) * HALF)])

    for copy in sent + in_copies + outs:
        copy.wait_send()
    for r in range(ROUNDS):
        for k in range(4):
            plane_copy(r, k).wait_send()
    for way in range(2):
        for j in range(15):
            cross_copy(way, j).wait_send()
    for copy in stores:
        copy.wait()


def finish(delta, error, params, momentum, left, right, ready, new_params, new_momentum, new_error, outputs):
    outputs[...] = ready[...]
    for h in range(2):
        cols = slice(h * HALF, (h + 1) * HALF)
        approx = jnp.dot(left[...], right[h], preferred_element_type=F32)
        merged = delta[0, :, cols].astype(F32) + error[0, :, cols].astype(F32)
        new_error[0, :, cols] = (merged - approx).astype(BF)
        m = 0.9 * momentum[:, cols] + approx
        new_momentum[:, cols] = m
        new_params[:, cols] = params[:, cols] - 0.7 * (approx + 0.9 * m)


def body(delta, error, params, momentum, q_init, inputs):
    dma = pltpu.SemaphoreType.DMA
    v = pltpu.VMEM
    anywhere = pl.BlockSpec(memory_space=pl.ANY)
    left, right, ready = pl.pallas_call(
        kernel,
        name="outer_step",
        out_shape=[
            jax.ShapeDtypeStruct((ROWS, 256), BF),
            jax.ShapeDtypeStruct((2, 256, HALF), BF),
            jax.ShapeDtypeStruct((512, 2560), BF),
        ],
        in_specs=[anywhere] * 6,
        out_specs=[anywhere] * 3,
        scratch_shapes=[
            v((5120, HALF), BF), v((2, 512, 5120), BF), v((2, 512, HALF), F32),
            v((ROWS, 2560), BF), v((ROWS, 2560), BF), v((ROWS, HALF), F32), v((ROWS, HALF), F32),
            v((64, 2560), F32), v((128, 2560), BF), v((2, 512, HALF), BF), v((512, HALF), BF),
            v((160, 128), F32), v((80, 128), F32), v((4, 80, 128), F32), v((160, 128), F32), v((ROWS, 256), BF),
            v((2, 16, 80, 128), BF), v((5120, 128), BF), v((2, 512, 256), BF),
            v((4, 32, 128), F32), v((4, 32, 128), F32), v((64, 128), F32), v((128, ROWS), BF),
            v((2, 64, HALF), F32), v((64, HALF), F32), v((64, HALF), F32), v((3, 16, HALF), F32), v((16, HALF), F32), v((16, HALF), F32),
            v((3, 8, 640), F32), v((4, 8, 640), F32), v((64, HALF), F32), v((2, 64, HALF), F32), v((2, 256, HALF), BF),
            dma((ROUNDS, 4)), dma((ROUNDS, 4)), dma((2, 15)), dma((2, 15)), dma((8,)), dma((8,)),
            dma((35,)), dma((35,)), dma((4,)), dma((4,)), dma((2,)), dma((2,)),
        ],
        compiler_params=pltpu.CompilerParams(collective_id=0, has_side_effects=True, vmem_limit_bytes=VMEM_MIB * 2**20),
        cost_estimate=pl.CostEstimate(flops=15 * 10**9, bytes_accessed=30 * 10**6, transcendentals=0),
    )(delta, error, params, momentum, q_init.T, inputs)
    lines = pl.BlockSpec((LINES, 2560), lambda i: (i, 0))
    columns = pl.BlockSpec((512, 8 * LINES), lambda i: (0, i))
    boxed = pl.BlockSpec((1, LINES, 2560), lambda i: (0, i, 0))
    return tuple(pl.pallas_call(
        finish,
        name="finish",
        grid=(ROWS // LINES,),
        out_shape=[
            jax.ShapeDtypeStruct((ROWS, 2560), F32),
            jax.ShapeDtypeStruct((ROWS, 2560), F32),
            jax.ShapeDtypeStruct((1, ROWS, 2560), BF),
            jax.ShapeDtypeStruct((512, 2560), BF),
        ],
        in_specs=[
            boxed, boxed, lines, lines, pl.BlockSpec((LINES, 256), lambda i: (i, 0)),
            pl.BlockSpec((2, 256, HALF), lambda i: (0, 0, 0)), columns,
        ],
        out_specs=[lines, lines, boxed, columns],
        compiler_params=pltpu.CompilerParams(vmem_limit_bytes=VMEM_MIB * 2**20),
        cost_estimate=pl.CostEstimate(flops=500 * 10**6, bytes_accessed=24 * 10**6, transcendentals=0),
    )(delta, error, params, momentum, left, right, ready))


def solution(mesh):
    in_specs = (
        P("island", "fsdp", None),
        P("island", "fsdp", None),
        P("fsdp", None),
        P("fsdp", None),
        P(),
        P(("island", "fsdp"), None),
    )
    out_specs = (
        P("fsdp", None),
        P("fsdp", None),
        P("island", "fsdp", None),
        P(("island", "fsdp"), None),
    )
    return jax.shard_map(body, mesh=mesh, in_specs=in_specs, out_specs=out_specs, check_vma=False)
```

```python
import jax
import jax.numpy as jnp
from jax import lax
from jax.experimental import pallas as pl
from jax.experimental.pallas import tpu as pltpu
from jax.sharding import PartitionSpec as P

BF = jnp.bfloat16
F32 = jnp.float32
MESH = pl.DeviceIdType.MESH

ROWS = 320
HALF = 1280
UNIT = 640
STREAM = 112
CROSS = 48
ROUNDS = 15
WIDTH = 640
VMEM_MIB = 60
OFFS = (0, -1, 1, 2)


def plan():
    table = [[None] * 4 for _ in range(ROUNDS)]
    for side, (h0, h1, back) in enumerate(((0, 1, -1), (1, 0, 1))):
        x, z = side, 2 + side
        table[0][x], table[1][x], table[2][x] = ("a", 0, 0, h0), ("a", 0, 0, h1), ("a", back, 0, h0)
        table[0][z], table[1][z], table[2][z] = ("b", 0, 0, h0), ("b", 0, 0, h1), ("b", 0, back, h0)
        for k, off in enumerate(OFFS):
            table[3 + 3 * k][x] = ("b", 0, off, h0)
            table[4 + 3 * k][x] = ("b", 0, off, h1)
            table[5 + 3 * k][x] = ("b", back, off, h0)
            table[3 + 2 * k][z] = ("a", off, 0, h0)
            table[4 + 2 * k][z] = ("a", off, 0, h1)
            table[11 + k][z] = ("a", off, back, h0)
    return table


TABLE = plan()
UP = [(1, -1, 0), (1, 1, 0), (2, 2, 0)]
for _k, _o in enumerate(OFFS):
    UP += [(4 + 2 * _k, _o, -1), (4 + 2 * _k, _o, 1)]
UP += [(11 + _k, _o, 2) for _k, _o in enumerate(OFFS)]
DOWN = [(1, 0, -1), (1, 0, 1), (2, 0, 2)]
for _k, _o in enumerate(OFFS):
    DOWN += [(4 + 3 * _k, -1, _o), (4 + 3 * _k, 1, _o), (5 + 3 * _k, 2, _o)]


def kernel(
    delta, error, params, momentum, q_init, inputs,
    left_out, right_out, outputs,
    wbuf, xin, acc, dl, er, prm, mom, q32, q2, obuf, sbuf,
    ploc, ph1, ph2, pk, p2cat, pgb, pfull, tcat,
    gx, gz, inverse, split, rloc, rin, racc, yin, s16, t16, xrs, zrs, rfull, wf, wcat,
    plane_send, plane_recv, cross_send, cross_recv, load, store,
    c_send, c_recv, in_send, in_recv, out_send, out_recv,
):
    i, f = lax.axis_index("island"), lax.axis_index("fsdp")
    y, c = i // 2, lax.rem(i, 2)
    z, x = f // 4, lax.rem(f, 4)
    parity = lax.rem(y, 2)
    u, v = x + c * (z - x), z + c * (x - z)

    def wrap(v):
        return lax.rem(v + 4, 4)

    def peer(dx=0, dy=0, dz=0, dc=0):
        return (wrap(y + dy) * 2 + lax.rem(c + dc, 2), wrap(z + dz) * 4 + wrap(x + dx))

    def along_u(d):
        return dict(dx=d * (1 - c), dz=d * c)

    def along_v(d):
        return dict(dx=d * c, dz=d * (1 - c))

    def shard(dx, dz):
        return wrap(z + dz) * 4 + wrap(x + dx)

    PEERS = [dict(dx=1), dict(dx=-1), dict(dx=2), dict(dy=1), dict(dy=-1), dict(dy=2),
             dict(dz=1), dict(dz=-1), dict(dz=2), dict(dc=1)]
    LINKS = [dict(dx=1), dict(dx=-1), dict(dz=1), dict(dz=-1)]

    barrier = pltpu.get_barrier_semaphore()
    for p in PEERS:
        pl.semaphore_signal(barrier, inc=1, device_id=peer(**p), device_id_type=MESH)

    def mine(col):
        return pl.ds(pl.multiple_of(col, 128), HALF)

    loads = {}

    def start_load(n, src, dst):
        loads[n] = pltpu.make_async_copy(src, dst, load.at[n])
        loads[n].start()

    start_load(0, params.at[:, mine(c * HALF)], prm)
    start_load(1, momentum.at[:, mine(c * HALF)], mom)
    start_load(2, q_init, q32)
    start_load(3, delta.at[0], dl)
    start_load(4, error.at[0], er)

    loads[0].wait()
    loads[1].wait()

    @pl.loop(0, ROWS // 32)
    def _(t):
        r = pl.ds(pl.multiple_of(t * 32, 32), 32)
        b = prm[r, :] - 0.567 * mom[r, :]
        wbuf[pl.ds(pl.multiple_of(f * ROWS + t * 32, 32), 32), :] = b.astype(BF)

    def swap(v):
        return pltpu.roll(v, 64, 1)

    def low(rows):
        return lax.broadcasted_iota(jnp.int32, (rows, 128), 1) < 64

    loads[2].wait()
    q = q32[...]
    hi = q.astype(BF)
    q2[0:64, :] = hi
    q2[64:128, :] = (q - hi.astype(F32)).astype(BF)
    loads[3].wait()
    loads[4].wait()
    last_dims = (((1,), (1,)), ((), ()))
    p_loc = lax.dot_general(dl[...], q2[...], last_dims, preferred_element_type=F32)
    p_loc = p_loc + lax.dot_general(er[...], q2[...], last_dims, preferred_element_type=F32)
    p_loc = p_loc + swap(p_loc)
    ploc[...] = jnp.where(low(160), p_loc[0:160], p_loc[160:320])

    pl.semaphore_wait(barrier, len(PEERS))

    sent = []

    def send(n, src, dst, **to):
        copy = pltpu.make_async_remote_copy(
            src_ref=src, dst_ref=dst, send_sem=c_send.at[n], recv_sem=c_recv.at[n],
            device_id=peer(**to), device_id_type=MESH)
        copy.start()
        sent.append(copy)

    def arrive(n, dst):
        pltpu.make_async_remote_copy(
            src_ref=dst, dst_ref=dst, send_sem=c_send.at[n], recv_sem=c_recv.at[n],
            device_id=peer(dc=1), device_id_type=MESH).wait_recv()

    TO = (1, -1, 2)

    def region(stream, dx, dz, h):
        row = shard(dx, dz) * ROWS + CROSS * parity + (0 if stream == "a" else 160)
        return wbuf.at[pl.ds(pl.multiple_of(row, 16), STREAM), pl.ds(h * UNIT, UNIT)]

    def plane_copy(r, k, arriving=False):
        stream, dx, dz, h = TABLE[r][k]
        if arriving:
            step = -1 if k % 2 == 0 else 1
            dx, dz = (dx + step, dz) if k < 2 else (dx, dz + step)
        here = region(stream, dx, dz, h)
        return pltpu.make_async_remote_copy(
            src_ref=here, dst_ref=here, send_sem=plane_send.at[r, k], recv_sem=plane_recv.at[r, k],
            device_id=peer(**LINKS[k]), device_id_type=MESH)

    def cross_copy(way, j, arriving=False):
        _, dx, dz = (UP, DOWN)[way][j]
        par = 1 - parity if arriving else parity
        row = shard(dx, dz) * ROWS + 160 * way + STREAM * par
        here = wbuf.at[pl.ds(pl.multiple_of(row, 16), CROSS), :]
        return pltpu.make_async_remote_copy(
            src_ref=here, dst_ref=here, send_sem=cross_send.at[way, j], recv_sem=cross_recv.at[way, j],
            device_id=peer(dy=1 if way == 0 else -1), device_id_type=MESH)

    def issue(r):
        for k in range(4):
            plane_copy(r, k).start()

    def cross(*js):
        for j in js:
            for way in range(2):
                cross_copy(way, j).start()

    def got(q):
        for k in range(4):
            plane_copy(q, k, arriving=True).wait_recv()

    def go(q, hold=False):
        if q + 2 < ROUNDS:
            issue(q + 2)
        if not hold:
            for way in range(2):
                for j, (need, _, _) in enumerate((UP, DOWN)[way]):
                    if need == q:
                        cross_copy(way, j).start()

    def crossed(way, *js):
        for j in js:
            cross_copy(way, j, arriving=True).wait_recv()

    def part(ref, k):
        return ref.at[pl.ds(pl.multiple_of(k * 80, 16), 80)]

    send(0, part(ploc, 1 - c), ph1, dc=1)
    issue(0)
    issue(1)
    start_load(5, inputs, xin.at[c])
    arrive(0, ph1)
    ph2[y] = part(ploc, c)[...] + ph1[...]
    for n, d in enumerate(TO):
        send(1 + n, ph2.at[y], ph2.at[y], dy=d)

    in_copies = []

    def feed(k):
        rows = xin.at[c, pl.ds(k * 128, 128)]
        copy = pltpu.make_async_remote_copy(
            src_ref=rows, dst_ref=rows, send_sem=in_send.at[k], recv_sem=in_recv.at[k],
            device_id=peer(dc=1), device_id_type=MESH)
        copy.start()
        in_copies.append(copy)

    def fed(k):
        rows = xin.at[1 - c, pl.ds(k * 128, 128)]
        pltpu.make_async_remote_copy(
            src_ref=rows, dst_ref=rows, send_sem=in_send.at[k], recv_sem=in_recv.at[k],
            device_id=peer(dc=1), device_id_type=MESH).wait_recv()

    loads[5].wait()
    feed(0)
    got(0)
    go(0)

    for n, d in enumerate(TO):
        arrive(1 + n, ph2.at[wrap(y - d)])
    mine_sum = (ph2[0] + ph2[1]) + (ph2[2] + ph2[3])
    part(pk, c)[...] = mine_sum
    own = v * 4 + u
    pgb[c, own] = mine_sum.astype(BF)
    send(4, part(pk, c), part(pk, c), dc=1)
    for n, d in enumerate(TO):
        send(5 + n, pgb.at[c, own], pgb.at[c, own], **along_u(d))
    arrive(4, part(pk, 1 - c))
    whole = pk[...]
    other = swap(whole)
    dup = jnp.concatenate([jnp.where(low(160), whole, other), jnp.where(low(160), other, whole)], axis=0)
    low320 = low(ROWS)
    hi = dup.astype(BF)
    lo = dup - hi.astype(F32)
    p2cat[:, 0:128] = hi
    p2cat[:, 128:256] = jnp.where(low320, lo, 0.0).astype(BF)
    gram = lax.dot_general(dup, dup, (((0,), (0,)), ((), ())), precision=lax.Precision.HIGHEST,
                           preferred_element_type=F32)
    gx[u] = jnp.where(low(32), gram[0:32], gram[32:64])
    for n, d in enumerate(TO):
        send(29 + n, gx.at[u], gx.at[u], **along_u(d))
    got(1)
    go(1, hold=True)
    cross(0)
    split[...] = jnp.where(low320, hi.astype(F32), lo).T.astype(BF)
    for h in range(2):
        for t in range(2):
            src = slice(h * HALF + t * 640, h * HALF + (t + 1) * 640)
            raw = jnp.dot(split[...], dl[:, src], preferred_element_type=F32)
            raw = raw + jnp.dot(split[...], er[:, src], preferred_element_type=F32)
            rloc[h, :, t * 640 : (t + 1) * 640] = raw[0:64] + raw[64:128]

    send(8, rloc.at[1 - c], rin, dc=1)
    feed(1)
    got(2)
    for n, d in enumerate(TO):
        arrive(29 + n, gx.at[wrap(u - d)])
    gz[v] = (gx[0] + gx[1]) + (gx[2] + gx[3])
    for n, d in enumerate(TO):
        send(32 + n, gz.at[v], gz.at[v], **along_v(d))
    for n, d in enumerate(TO):
        arrive(5 + n, pgb.at[c, v * 4 + wrap(u - d)])
    row4 = pl.ds(v * 4, 4)
    for n, d in enumerate(TO):
        send(9 + n, pgb.at[c, row4], pgb.at[c, row4], **along_v(d))
    go(2, hold=True)
    arrive(8, rin)
    racc[...] = rloc[c] + rin[...]

    def rows16(k):
        return pl.ds(pl.multiple_of(k * 16, 16), 16)

    for n, d in enumerate(TO):
        send(12 + n, racc.at[rows16(wrap(y + d))], yin.at[n], dy=d)
    cross(1, 2)
    feed(2)
    feed(3)
    got(3)
    for n, d in enumerate(TO):
        arrive(32 + n, gz.at[wrap(v - d)])
    gram = (gz[0] + gz[1]) + (gz[2] + gz[3])
    go(3)

    lane64 = lax.broadcasted_iota(jnp.int32, (64, 128), 1)
    sub64 = lax.broadcasted_iota(jnp.int32, (64, 128), 0)
    a = jnp.concatenate([gram, swap(gram)], axis=0)
    a = jnp.where(lane64 < 64, a, jnp.where(lane64 == sub64 + 64, 1.0, 0.0))

    def eliminate(a, first, end):
        for k in range(first, end):
            row = a[k : k + 1, :] / a[k : k + 1, k : k + 1]
            a = jnp.where(sub64 == k, row, a - a[:, k : k + 1] * row)
        return a

    a = eliminate(a, 0, 32)
    got(4)
    for n, d in enumerate(TO):
        arrive(9 + n, pgb.at[c, pl.ds(wrap(v - d) * 4, 4)])
    send(24, pgb.at[c], pgb.at[c], dc=1)
    go(4)
    a = eliminate(a, 32, 64)
    inverse[...] = swap(a)
    got(5)
    for n in range(3):
        arrive(12 + n, yin.at[n])
    s16[...] = (racc[rows16(y), :] + yin[0]) + (yin[1] + yin[2])

    def block(ref, k):
        return ref.at[pl.ds(pl.multiple_of((k // 2) * 8, 8), 8), pl.ds(pl.multiple_of(lax.rem(k, 2) * 640, 128), 640)]

    for n, d in enumerate(TO):
        send(15 + n, block(s16, wrap(u + d)), xrs.at[n], **along_u(d))
    go(5)

    arrive(24, pgb.at[1 - c])

    @pl.loop(0, 16)
    def _(t):
        for h in range(2):
            two = pgb[h, t]
            at = (t if h == 0 else lax.rem(t, 4) * 4 + t // 4) * ROWS + h * 80
            pfull[pl.ds(pl.multiple_of(at, 16), 80), :] = two
            pfull[pl.ds(pl.multiple_of(at + 160, 16), 80), :] = swap(two.astype(F32)).astype(BF)

    low512 = low(512)

    def left(m):
        part_m = jnp.dot(xin[m], pfull[...], preferred_element_type=F32) * -1.33
        part_m = jnp.where(low512, part_m, swap(part_m))
        hi = part_m.astype(BF)
        tcat[m, :, 0:128] = hi
        tcat[m, :, 128:256] = jnp.where(low512, part_m - hi.astype(F32), 0.0).astype(BF)

    def product(row, depth, m, first=False):
        ks = pl.ds(pl.multiple_of(row, 128), depth)
        term = jnp.dot(xin[m, :, ks], wbuf[ks, :], preferred_element_type=F32)
        if first:
            acc[m] = term
        else:
            acc[m] += term

    for k in range(4):
        fed(k)
    got(6)
    for n in range(3):
        arrive(15 + n, xrs.at[n])
    zrs[v] = (block(s16, u)[...] + xrs[0]) + (xrs[1] + xrs[2])
    for n, d in enumerate(TO):
        send(18 + n, zrs.at[v], zrs.at[v], **along_v(d))
    go(6)
    left(0)
    got(7)
    for n, d in enumerate(TO):
        arrive(18 + n, zrs.at[wrap(v - d)])
    block(t16, u)[...] = (zrs[0] + zrs[1]) + (zrs[2] + zrs[3])
    for n, d in enumerate(TO):
        send(21 + n, block(t16, u), block(t16, u), **along_u(d))
    go(7)
    left(1)
    got(8)
    for n, d in enumerate(TO):
        arrive(21 + n, block(t16, wrap(u - d)))
    rfull[rows16(y), :] = t16[...]
    for n, d in enumerate(TO):
        send(25 + n, rfull.at[rows16(y)], rfull.at[rows16(y)], dy=d)
    go(8)
    crossed(0, 0, 1, 2)
    crossed(1, 3, 4, 5)
    product(z * 1280, 1280, 0, first=True)
    got(9)
    go(9)
    product(z * 1280, 1280, 1, first=True)
    got(10)
    go(10)
    for n, d in enumerate(TO):
        arrive(25 + n, rfull.at[rows16(wrap(y - d))])

    wf[c] = jnp.dot(inverse[:, 0:64], rfull[...], precision=lax.Precision.HIGHEST, preferred_element_type=F32) * 0.125
    send(28, wf.at[c], wf.at[c], dc=1)
    got(11)
    go(11)
    arrive(28, wf.at[1 - c])
    for h in range(2):
        w = wf[h]
        hi = w.astype(BF)
        wcat[h, 0:64, :] = hi
        wcat[h, 64:128, :] = (w - hi.astype(F32)).astype(BF)
        wcat[h, 128:192, :] = hi
        wcat[h, 192:256, :] = jnp.zeros((64, HALF), BF)
    stores = []

    def start_store(src, dst):
        copy = pltpu.make_async_copy(src, dst, store.at[len(stores)])
        copy.start()
        stores.append(copy)

    start_store(p2cat, left_out)
    start_store(wcat, right_out)

    @pl.loop(0, 2)
    def _(m):
        acc[m] += jnp.dot(tcat[m], wcat[c], preferred_element_type=F32)

    got(12)
    go(12)
    crossed(0, 3, 5, 7, 9)
    crossed(1, 0, 6, 7, 8)
    product(wrap(z - 1) * 1280, 1280, 0)
    product(wrap(z - 1) * 1280, 1280, 1)
    got(13)
    go(13)
    crossed(0, 4, 6, 8, 10)
    crossed(1, 1, 9, 10, 11)
    product(wrap(z + 1) * 1280, 1280, 0)
    got(14)
    go(14)
    product(wrap(z + 1) * 1280, 1280, 1)

    crossed(0, 11, 12, 13)
    crossed(1, 2, 12, 13)
    last = wrap(z + 2) * 1280
    pair = x // 2
    for m in range(2):
        product(last + pair * 640, 640, m)
    crossed(0, 14)
    crossed(1, 14)
    ks = pl.ds(pl.multiple_of(last + (1 - pair) * 640, 128), 640)

    def final(m, t):
        rows = slice(t * 256, (t + 1) * 256)
        return (acc[m, rows, :] + jnp.dot(xin[m, rows, ks], wbuf[ks, :], preferred_element_type=F32)).astype(BF)

    outs = []
    for t in range(2):
        rows = pl.ds(t * 256, 256)
        sbuf[t * 256 : (t + 1) * 256, :] = final(1 - c, t)
        copy = pltpu.make_async_remote_copy(
            src_ref=sbuf.at[rows], dst_ref=obuf.at[c, rows],
            send_sem=out_send.at[t], recv_sem=out_recv.at[t], device_id=peer(dc=1), device_id_type=MESH)
        copy.start()
        outs.append(copy)
    for t in range(2):
        obuf[c, t * 256 : (t + 1) * 256, :] = final(c, t)
    start_store(obuf.at[c], outputs.at[:, mine(c * HALF)])
    for t in range(2):
        there = obuf.at[1 - c, pl.ds(t * 256, 256)]
        pltpu.make_async_remote_copy(
            src_ref=there, dst_ref=there, send_sem=out_send.at[t], recv_sem=out_recv.at[t],
            device_id=peer(dc=1), device_id_type=MESH).wait_recv()
    start_store(obuf.at[1 - c], outputs.at[:, mine((1 - c) * HALF)])

    for copy in sent + in_copies + outs:
        copy.wait_send()
    for r in range(ROUNDS):
        for k in range(4):
            plane_copy(r, k).wait_send()
    for way in range(2):
        for j in range(15):
            cross_copy(way, j).wait_send()
    for copy in stores:
        copy.wait()


def finish(delta, error, params, momentum, left, right, ready, new_params, new_momentum, new_error, outputs):
    outputs[...] = ready[...]
    approx = jnp.dot(left[...], right[0], preferred_element_type=F32)
    merged = delta[0].astype(F32) + error[0].astype(F32)
    new_error[0] = (merged - approx).astype(BF)
    m = 0.9 * momentum[...] + approx
    new_momentum[...] = m
    new_params[...] = params[...] - 0.7 * (approx + 0.9 * m)


def body(delta, error, params, momentum, q_init, inputs):
    dma = pltpu.SemaphoreType.DMA
    v = pltpu.VMEM
    anywhere = pl.BlockSpec(memory_space=pl.ANY)
    left, right, ready = pl.pallas_call(
        kernel,
        name="outer_step",
        out_shape=[
            jax.ShapeDtypeStruct((ROWS, 256), BF),
            jax.ShapeDtypeStruct((2, 256, HALF), BF),
            jax.ShapeDtypeStruct((512, 2560), BF),
        ],
        in_specs=[anywhere] * 6,
        out_specs=[anywhere] * 3,
        scratch_shapes=[
            v((5120, HALF), BF), v((2, 512, 5120), BF), v((2, 512, HALF), F32),
            v((ROWS, 2560), BF), v((ROWS, 2560), BF), v((ROWS, HALF), F32), v((ROWS, HALF), F32),
            v((64, 2560), F32), v((128, 2560), BF), v((2, 512, HALF), BF), v((512, HALF), BF),
            v((160, 128), F32), v((80, 128), F32), v((4, 80, 128), F32), v((160, 128), F32), v((ROWS, 256), BF),
            v((2, 16, 80, 128), BF), v((5120, 128), BF), v((2, 512, 256), BF),
            v((4, 32, 128), F32), v((4, 32, 128), F32), v((64, 128), F32), v((128, ROWS), BF),
            v((2, 64, HALF), F32), v((64, HALF), F32), v((64, HALF), F32), v((3, 16, HALF), F32), v((16, HALF), F32), v((16, HALF), F32),
            v((3, 8, 640), F32), v((4, 8, 640), F32), v((64, HALF), F32), v((2, 64, HALF), F32), v((2, 256, HALF), BF),
            dma((ROUNDS, 4)), dma((ROUNDS, 4)), dma((2, 15)), dma((2, 15)), dma((8,)), dma((8,)),
            dma((35,)), dma((35,)), dma((4,)), dma((4,)), dma((2,)), dma((2,)),
        ],
        compiler_params=pltpu.CompilerParams(collective_id=0, has_side_effects=True, vmem_limit_bytes=VMEM_MIB * 2**20),
        cost_estimate=pl.CostEstimate(flops=15 * 10**9, bytes_accessed=30 * 10**6, transcendentals=0),
    )(delta, error, params, momentum, q_init.T, inputs)
    steps = HALF // WIDTH
    lines = pl.BlockSpec((ROWS, WIDTH), lambda i: (0, i))
    columns = pl.BlockSpec((512, WIDTH), lambda i: (0, i))
    boxed = pl.BlockSpec((1, ROWS, WIDTH), lambda i: (0, 0, i))
    return tuple(pl.pallas_call(
        finish,
        name="finish",
        grid=(2 * steps,),
        out_shape=[
            jax.ShapeDtypeStruct((ROWS, 2560), F32),
            jax.ShapeDtypeStruct((ROWS, 2560), F32),
            jax.ShapeDtypeStruct((1, ROWS, 2560), BF),
            jax.ShapeDtypeStruct((512, 2560), BF),
        ],
        in_specs=[
            boxed, boxed, lines, lines, pl.BlockSpec((ROWS, 256), lambda i: (0, 0)),
            pl.BlockSpec((1, 256, WIDTH), lambda i: (i // steps, 0, i % steps)), columns,
        ],
        out_specs=[lines, lines, boxed, columns],
        compiler_params=pltpu.CompilerParams(vmem_limit_bytes=VMEM_MIB * 2**20),
        cost_estimate=pl.CostEstimate(flops=500 * 10**6, bytes_accessed=24 * 10**6, transcendentals=0),
    )(delta, error, params, momentum, left, right, ready))


def solution(mesh):
    in_specs = (
        P("island", "fsdp", None),
        P("island", "fsdp", None),
        P("fsdp", None),
        P("fsdp", None),
        P(),
        P(("island", "fsdp"), None),
    )
    out_specs = (
        P("fsdp", None),
        P("fsdp", None),
        P("island", "fsdp", None),
        P(("island", "fsdp"), None),
    )
    return jax.shard_map(body, mesh=mesh, in_specs=in_specs, out_specs=out_specs, check_vma=False)
```
